128 devices in a mesh: lat: 32 (over x, z, core), lon: 4 (over y).
Axes of the slice: x: 4, y: 4, z: 4, core: 2. Of those that a mesh axis runs over, the one named last changes fastest.
Arguments:
- grid_fields: bfloat16 [32, 4, 2048, 227], P('lat', 'lon'), may hold values from -6 to 6
- mesh_static: bfloat16 [32, 4, 512, 512], P('lat', 'lon'), may hold values from -6 to 6
- encode_senders: int32 [32, 4, 3072], P('lat', 'lon'), may hold values from 0 to 16639, as said below
- encode_receivers: int32 [32, 4, 3072], P('lat', 'lon'), may hold values from 0 to 511
- encode_geometry: float32 [32, 4, 4, 3072], P('lat', 'lon'), may hold values from -6 to 6
- encode_valid: int32 [32, 4], P('lat', 'lon'), may hold values from 1536 to 3072, as said below
- mesh_senders: int32 [32, 4, 4096], P('lat', 'lon'), may hold values from 0 to 4607
- mesh_receivers: int32 [32, 4, 4096], P('lat', 'lon'), may hold values from 0 to 511
- mesh_geometry: float32 [32, 4, 4, 4096], P('lat', 'lon'), may hold values from -6 to 6
- mesh_valid: int32 [32, 4], P('lat', 'lon'), may hold values from 2048 to 4096, as said below
- decode_senders: int32 [32, 4, 3, 2048], P('lat', 'lon'), may hold values from 0 to 4607
- embed_weight: bfloat16 [227, 512], replicated, may hold values from -0.375 to 0.375
- encode_source: bfloat16 [512, 512], replicated, may hold values from -0.25 to 0.25
- encode_edge: float32 [4, 512], replicated, may hold values from -3 to 3
- encode_second: bfloat16 [512, 512], replicated, may hold values from -0.25 to 0.25
- node_first: bfloat16 [512, 512], replicated, may hold values from -0.25 to 0.25
- node_second: bfloat16 [512, 512], replicated, may hold values from -0.25 to 0.25
- node_gain: float32 [512], replicated, may hold values from 0.1 to 1.9
- process_source: bfloat16 [512, 512], replicated, may hold values from -0.25 to 0.25
- process_target: bfloat16 [512, 512], replicated, may hold values from -0.25 to 0.25
- process_edge: float32 [4, 512], replicated, may hold values from -3 to 3
- process_second: bfloat16 [512, 512], replicated, may hold values from -0.25 to 0.25
- update_message: bfloat16 [512, 512], replicated, may hold values from -0.25 to 0.25
- update_state: bfloat16 [512, 512], replicated, may hold values from -0.25 to 0.25
- update_out: bfloat16 [512, 512], replicated, may hold values from -0.25 to 0.25
- process_gain: float32 [512], replicated, may hold values from 0.1 to 1.9
- decode_source: bfloat16 [512, 512], replicated, may hold values from -0.25 to 0.25
- decode_target: bfloat16 [512, 512], replicated, may hold values from -0.25 to 0.25
- decode_hidden: bfloat16 [512, 512], replicated, may hold values from -0.25 to 0.25
- output_weight: bfloat16 [512, 227], replicated, may hold values from -0.25 to 0.25
Outputs:
- prediction: float32 [32, 4, 2048, 227], P('lat', 'lon')
The draws below stay inside these ranges and needn't reach their ends.
Inputs may be any that keep to these rules, and one draw needn't show every extreme that they name: `encode_senders`: a sender outside the own block (rows 8192 to 10239) is one of the first 256 cells of its block; every device has an edge at cell 256 - 1 of each of its eight neighbouring blocks and one at cell 0 of the first neighbouring block. `encode_valid`: valid slots are the first ones of a device; the first device fills all 3072. `mesh_valid`: valid slots are the first ones of a device; the first device fills all 4096.
All inputs are finite; a program needn't handle non-finite values.
Results may differ from the reference program's by a relative error of at most 0.017.
Values may be sent and summed in bfloat16 or wider, within the bound.
No kernel may reach another device: no remote copies, remote signals or barrier semaphores. Data moves between devices by JAX's collectives and lax.ppermute only.
A program may use at most 128 MiB of HBM per device.

```python
import jax
import jax.numpy as jnp
from jax import lax

C = 227
L = 512
G_DEV = 2048
M_DEV = 512
FEAT = 4
E_G = 3072
E_M = 4096
N_LAT = 32
N_LON = 4


def draw_encode_senders(key, part):
    key = jax.random.fold_in(key, 13)
    own_key, strip_key = jax.random.split(key)
    shape = (N_LAT, N_LON, E_G)
    strip = G_DEV // 8
    own_cells = jax.random.randint(own_key, shape, 0, G_DEV)
    strip_cells = jax.random.randint(strip_key, shape, 0, strip)
    slots = jnp.arange(E_G, dtype=jnp.int32)
    forced = (slots % 2 == 1) & (slots < 16)
    strip_cells = jnp.where(forced[None, None, :], strip - 1, strip_cells)
    strip_cells = jnp.where((slots == 17)[None, None, :], 0, strip_cells)
    turn = slots // 2 % 8
    neighbour = jnp.where(turn >= 4, turn + 1, turn)
    crossing = neighbour[None, None, :] * G_DEV + strip_cells
    own = 4 * G_DEV + own_cells
    return jnp.where((slots % 2 == 0)[None, None, :], own, crossing).astype(jnp.int32)


def draw_encode_valid(key, part):
    key = jax.random.fold_in(key, 11)
    counts = jax.random.randint(key, (N_LAT, N_LON), E_G // 2, E_G + 1)
    return counts.at[0, 0].set(E_G).astype(jnp.int32)


def draw_mesh_valid(key, part):
    key = jax.random.fold_in(key, 12)
    counts = jax.random.randint(key, (N_LAT, N_LON), E_M // 2, E_M + 1)
    return counts.at[0, 0].set(E_M).astype(jnp.int32)


def with_ends(values, key, low, largest):
    longest = values.shape.index(max(values.shape))
    spots = []
    for shift in (0, 1):
        where = [jax.random.randint(jax.random.fold_in(key, axis), (), 0, length) for axis, length in enumerate(values.shape)]
        where[longest] = (where[longest] + shift) % values.shape[longest]
        spots.append(tuple(where))
    return values.at[spots[0]].set(low).at[spots[1]].set(largest)


def levels(rng, extent, cuts, least, high):
    def one(dim, parts):
        heights = jax.random.uniform(jax.random.fold_in(jax.random.fold_in(rng, 6), dim), (parts,), jnp.float32, least / len(cuts), high / len(cuts))
        return jnp.repeat(jnp.exp(heights), extent[dim] // parts).reshape((-1,) + (1,) * (len(extent) - dim - 1))

    level = one(*cuts[0])
    for cut in cuts[1:]:
        level = level * one(*cut)
    return level


def normal_values(rng, shape, width, most, pieces=(), kind=jnp.bfloat16):
    values = width * jax.random.normal(rng, shape, jnp.float32)
    if pieces:
        values = values * levels(rng, shape, pieces, -0.22, 0.18)
    return jnp.clip(values, -most, most).astype(kind)


def setup_inputs(seed: int = 0) -> dict:
    key_list = jax.random.split(jax.random.key(seed), 31)
    grid_fields = normal_values(key_list[0], (N_LAT, N_LON, G_DEV, C), 1.0, 6.0, ((0, 32), (1, 4)))
    mesh_static = normal_values(key_list[1], (N_LAT, N_LON, M_DEV, L), 1.0, 6.0, ((0, 32), (1, 4)))
    encode_senders = draw_encode_senders(jax.random.fold_in(key_list[30], 71), 0)
    encode_receivers = with_ends(jax.random.randint(key_list[3], (N_LAT, N_LON, E_G), 0, M_DEV), jax.random.fold_in(key_list[3], 1), 0, M_DEV - 1).astype(jnp.int32)
    encode_geometry = normal_values(key_list[4], (N_LAT, N_LON, FEAT, E_G), 1.0, 6.0, ((0, 32), (1, 4)), jnp.float32)
    encode_valid = draw_encode_valid(jax.random.fold_in(key_list[30], 71), 0)
    mesh_senders = with_ends(jax.random.randint(key_list[6], (N_LAT, N_LON, E_M), 0, 9 * M_DEV), jax.random.fold_in(key_list[6], 1), 0, (9 * M_DEV) - 1).astype(jnp.int32)
    mesh_receivers = with_ends(jax.random.randint(key_list[7], (N_LAT, N_LON, E_M), 0, M_DEV), jax.random.fold_in(key_list[7], 1), 0, M_DEV - 1).astype(jnp.int32)
    mesh_geometry = normal_values(key_list[8], (N_LAT, N_LON, FEAT, E_M), 1.0, 6.0, ((0, 32), (1, 4)), jnp.float32)
    mesh_valid = draw_mesh_valid(jax.random.fold_in(key_list[30], 71), 0)
    decode_senders = with_ends(jax.random.randint(key_list[10], (N_LAT, N_LON, 3, G_DEV), 0, 9 * M_DEV), jax.random.fold_in(key_list[10], 1), 0, (9 * M_DEV) - 1).astype(jnp.int32)
    embed_weight = normal_values(key_list[11], (C, L), C ** -0.5, 0.375)
    encode_source = normal_values(key_list[12], (L, L), L ** -0.5, 0.25)
    encode_edge = normal_values(key_list[13], (FEAT, L), FEAT ** -0.5, 3.0, (), jnp.float32)
    encode_second = normal_values(key_list[14], (L, L), L ** -0.5, 0.25)
    node_first = normal_values(key_list[15], (L, L), L ** -0.5, 0.25)
    node_second = normal_values(key_list[16], (L, L), L ** -0.5, 0.25)
    node_gain = jnp.clip(1.0 + 0.18 * jax.random.normal(key_list[17], (L,), jnp.float32), 0.1, 1.9)
    process_source = normal_values(key_list[18], (L, L), L ** -0.5, 0.25)
    process_target = normal_values(key_list[19], (L, L), L ** -0.5, 0.25)
    process_edge = normal_values(key_list[20], (FEAT, L), FEAT ** -0.5, 3.0, (), jnp.float32)
    process_second = normal_values(key_list[21], (L, L), L ** -0.5, 0.25)
    update_message = normal_values(key_list[22], (L, L), L ** -0.5, 0.25)
    update_state = normal_values(key_list[23], (L, L), L ** -0.5, 0.25)
    update_out = normal_values(key_list[24], (L, L), L ** -0.5, 0.25)
    process_gain = jnp.clip(1.0 + 0.18 * jax.random.normal(key_list[25], (L,), jnp.float32), 0.1, 1.9)
    decode_source = normal_values(key_list[26], (L, L), L ** -0.5, 0.25)
    decode_target = normal_values(key_list[27], (L, L), L ** -0.5, 0.25)
    decode_hidden = normal_values(key_list[28], (L, L), L ** -0.5, 0.25)
    output_weight = normal_values(key_list[29], (L, C), L ** -0.5, 0.25)
    return dict(grid_fields=grid_fields, mesh_static=mesh_static, encode_senders=encode_senders, encode_receivers=encode_receivers, encode_geometry=encode_geometry, encode_valid=encode_valid, mesh_senders=mesh_senders, mesh_receivers=mesh_receivers, mesh_geometry=mesh_geometry, mesh_valid=mesh_valid, decode_senders=decode_senders, embed_weight=embed_weight, encode_source=encode_source, encode_edge=encode_edge, encode_second=encode_second, node_first=node_first, node_second=node_second, node_gain=node_gain, process_source=process_source, process_target=process_target, process_edge=process_edge, process_second=process_second, update_message=update_message, update_state=update_state, update_out=update_out, process_gain=process_gain, decode_source=decode_source, decode_target=decode_target, decode_hidden=decode_hidden, output_weight=output_weight)


EPSILON = 1e-05

def layer_norm(values, gain):
    centre = values - lax.optimization_barrier(jnp.mean(values, axis=-1, keepdims=True))
    spread = lax.optimization_barrier(jnp.mean(centre * centre, axis=-1, keepdims=True))
    return centre * lax.rsqrt(spread + EPSILON) * gain

def geometry_term(geometry, weight):
    return jnp.einsum('fe,fl->el', geometry, weight, precision=lax.Precision.HIGHEST)

def neighbour_rows(table, lat_index, lon_index, senders):
    count_rows = table.shape[2]
    block = senders // count_rows
    offset = senders % count_rows
    source_lat = lat_index + block // 3 - 1
    source_lon = (lon_index + block % 3 - 1) % N_LON
    inside = (source_lat >= 0) & (source_lat < N_LAT)
    picked = table[jnp.clip(source_lat, 0, N_LAT - 1), source_lon, offset]
    return jnp.where(inside[..., None], picked, jnp.zeros((), table.dtype))

def collect(receivers, messages, nodes):
    onehot = (receivers[None, :] == jnp.arange(nodes, dtype=jnp.int32)[:, None]).astype(jnp.bfloat16)
    return jnp.dot(onehot, messages, preferred_element_type=jnp.float32)

def edge_messages(rows, geometry, edge_weight, second, valid):
    hidden = jax.nn.silu(rows + geometry_term(geometry, edge_weight)).astype(jnp.bfloat16)
    keep = jnp.arange(hidden.shape[0], dtype=jnp.int32) < valid
    product = jnp.dot(hidden, second, preferred_element_type=jnp.float32)
    return jnp.where(keep[:, None], product, jnp.zeros((), jnp.float32)).astype(jnp.bfloat16)

def reference(grid_fields, mesh_static, encode_senders, encode_receivers, encode_geometry, encode_valid, mesh_senders, mesh_receivers, mesh_geometry, mesh_valid, decode_senders, embed_weight, encode_source, encode_edge, encode_second, node_first, node_second, node_gain, process_source, process_target, process_edge, process_second, update_message, update_state, update_out, process_gain, decode_source, decode_target, decode_hidden, output_weight):
    devices = N_LAT * N_LON

    def flat(array):
        return array.reshape((devices,) + array.shape[2:])
    places = jnp.arange(devices, dtype=jnp.int32)
    embedded = jax.nn.silu(jnp.dot(grid_fields, embed_weight, preferred_element_type=jnp.float32)).astype(jnp.bfloat16)
    source_grid = jnp.dot(embedded, encode_source, preferred_element_type=jnp.float32).astype(jnp.bfloat16)

    def encode_one(item):
        place, senders, receivers, geometry, valid = item
        rows = neighbour_rows(source_grid, place // N_LON, place % N_LON, senders).astype(jnp.float32)
        messages = edge_messages(rows, geometry, encode_edge, encode_second, valid)
        return collect(receivers, messages, M_DEV)
    gathered = lax.map(encode_one, (places, flat(encode_senders), flat(encode_receivers), flat(encode_geometry), encode_valid.reshape(devices)))
    gathered = gathered.reshape(N_LAT, N_LON, M_DEV, L)
    node_hidden = jax.nn.silu(jnp.dot(gathered.astype(jnp.bfloat16), node_first, preferred_element_type=jnp.float32)).astype(jnp.bfloat16)
    mesh_start = (mesh_static.astype(jnp.float32) + layer_norm(jnp.dot(node_hidden, node_second, preferred_element_type=jnp.float32), node_gain)).astype(jnp.bfloat16)
    source_mesh = jnp.dot(mesh_start, process_source, preferred_element_type=jnp.float32).astype(jnp.bfloat16)

    def process_one(item):
        place, senders, receivers, geometry, valid, state = item
        target_mesh = jnp.dot(state, process_target, preferred_element_type=jnp.float32)
        rows = neighbour_rows(source_mesh, place // N_LON, place % N_LON, senders).astype(jnp.float32) + target_mesh[receivers]
        messages = edge_messages(rows, geometry, process_edge, process_second, valid)
        total = collect(receivers, messages, M_DEV).astype(jnp.bfloat16)
        update = jax.nn.silu(jnp.dot(total, update_message, preferred_element_type=jnp.float32) + jnp.dot(state, update_state, preferred_element_type=jnp.float32)).astype(jnp.bfloat16)
        normed = layer_norm(jnp.dot(update, update_out, preferred_element_type=jnp.float32), process_gain)
        return (state.astype(jnp.float32) + normed).astype(jnp.bfloat16)
    mesh_end = lax.map(process_one, (places, flat(mesh_senders), flat(mesh_receivers), flat(mesh_geometry), mesh_valid.reshape(devices), flat(mesh_start)))
    mesh_end = mesh_end.reshape(N_LAT, N_LON, M_DEV, L)
    source_out = jnp.dot(mesh_end, decode_source, preferred_element_type=jnp.float32).astype(jnp.bfloat16)

    def decode_one(item):
        place, senders, fields, local = item
        target_grid = jnp.dot(local, decode_target, preferred_element_type=jnp.float32)
        rows = neighbour_rows(source_out, place // N_LON, place % N_LON, senders).astype(jnp.float32) + target_grid[None]
        decode_edge = jax.nn.silu(rows).astype(jnp.bfloat16)
        decode_sum = lax.optimization_barrier(jnp.sum(decode_edge.astype(jnp.float32), axis=0)).astype(jnp.bfloat16)
        decode_final = jax.nn.silu(jnp.dot(decode_sum, decode_hidden, preferred_element_type=jnp.float32)).astype(jnp.bfloat16)
        return fields.astype(jnp.float32) + jnp.dot(decode_final, output_weight, preferred_element_type=jnp.float32)
    prediction = lax.map(decode_one, (places, flat(decode_senders), flat(grid_fields), flat(embedded)))
    return prediction.reshape(N_LAT, N_LON, G_DEV, C)
```

```python
import functools

import jax
import jax.numpy as jnp
from jax import lax
from jax.experimental import pallas as pl
from jax.experimental.pallas import tpu as pltpu
from jax.sharding import PartitionSpec as P

EPSILON = 1e-05
BF16 = jnp.bfloat16
F32 = jnp.float32
LANES = 128
VMEM_BYTES = 56 * 1024 * 1024

VMEM = pl.BlockSpec(memory_space=pltpu.VMEM)
SMEM = pl.BlockSpec(memory_space=pltpu.SMEM)
ANY = pl.BlockSpec(memory_space=pl.ANY)


def params():
    return pltpu.CompilerParams(vmem_limit_bytes=VMEM_BYTES)


def cost(flops, moved):
    return pl.CostEstimate(flops=flops, bytes_accessed=moved, transcendentals=0)


def silu(values):
    half = 0.5 * values
    return half + half * jnp.tanh(half)


def layer_norm(values, gain):
    centre = values - jnp.mean(values, axis=-1, keepdims=True)
    spread = jnp.mean(centre * centre, axis=-1, keepdims=True)
    return centre * lax.rsqrt(spread + EPSILON) * gain


def dot(a, b):
    return jnp.dot(a, b, preferred_element_type=F32)


def dot_rows(a, b):
    return lax.dot_general(a, b, (((0,), (0,)), ((), ())), preferred_element_type=F32)


def put_table(ref, first, values):
    parts = values.shape[1] // LANES
    for part in range(parts):
        ref[pl.ds(first * parts + part, values.shape[0], stride=parts), :] = values[
            :, part * LANES : (part + 1) * LANES
        ]


def gather(index, first, count, table, rows, parts, unroll=32):
    def body(step, carry):
        for slot in range(unroll):
            edge = step * unroll + slot
            start = pl.multiple_of(index[first + edge], parts)
            rows[pl.ds(pl.multiple_of(edge * parts, parts), parts), :] = table[
                pl.ds(start, parts), :
            ]
        return carry

    lax.fori_loop(0, count // unroll, body, 0)


def onehot(receivers, nodes):
    ids = lax.broadcasted_iota(jnp.int32, (nodes, receivers.shape[1]), 0)
    return jnp.where(ids == receivers, 1.0, 0.0).astype(BF16)


def own_kernel(fields, embed_weight, source_weight, embedded, table):
    values = silu(dot(fields[...], embed_weight[...])).astype(BF16)
    embedded[...] = values
    put_table(table, 0, dot(values, source_weight[...]).astype(BF16).astype(F32))


def embed_own(fields, embed_weight, source_weight):
    cells, channels = fields.shape
    width = embed_weight.shape[1]
    parts = width // LANES
    tile = 512
    return pl.pallas_call(
        own_kernel,
        grid=(cells // tile,),
        in_specs=[
            pl.BlockSpec((tile, channels), lambda i: (i, 0)),
            pl.BlockSpec((channels, width), lambda i: (0, 0)),
            pl.BlockSpec((width, width), lambda i: (0, 0)),
        ],
        out_specs=[
            pl.BlockSpec((tile, width), lambda i: (i, 0)),
            pl.BlockSpec((tile * parts, LANES), lambda i: (i, 0)),
        ],
        out_shape=[
            jax.ShapeDtypeStruct((cells, width), BF16),
            jax.ShapeDtypeStruct((cells * parts, LANES), F32),
        ],
        compiler_params=params(),
        cost_estimate=cost(2 * cells * width * (width + 256), 8 * 2**20),
    )(fields, embed_weight, source_weight)


def encode_kernel(
    index, strip_w, strip_e, strip_o, strip_n, strip_oc, strip_nc, own_table, receivers,
    geometry, edge_weight, embed_weight, source_weight, second, first_weight, node_second,
    gain, static, next_source, mesh_start, next_table,
    table, rows, total, wide, own_sem,
):
    cells = own_table.shape[0]
    parts = second.shape[0] // LANES
    copy = pltpu.make_async_copy(own_table, table.at[pl.ds(0, cells)], own_sem)
    copy.start()
    strips = [strip_w[...], strip_e[...], strip_o[...], strip_n[...]]
    strips += [strip_oc[0], strip_oc[1], strip_nc[0], strip_nc[1]]
    for slot, strip in enumerate(strips):
        values = silu(dot(strip, embed_weight[...])).astype(BF16)
        values = dot(values, source_weight[...]).astype(BF16).astype(F32)
        put_table(table, cells // parts + slot * strip.shape[0], values)
    copy.wait()
    edges = receivers.shape[1]
    gather(index, 0, edges, table, rows, parts)
    total[...] = jnp.zeros_like(total)
    tile = 512

    def step(i, carry):
        begin = pl.multiple_of(i * tile, tile)
        shift = dot_rows(geometry[:, pl.ds(begin, tile)], edge_weight[...])
        hidden = [
            silu(
                rows[pl.ds(begin * parts + part, tile, stride=parts), :]
                + shift[:, part * LANES : (part + 1) * LANES]
            ).astype(BF16)
            for part in range(parts)
        ]
        picks = onehot(receivers[:, pl.ds(begin, tile)], total.shape[0])
        total[...] += dot(picks, jnp.concatenate(hidden, axis=1))
        return carry

    lax.fori_loop(0, edges // tile, step, 0)
    gathered = dot(total[...].astype(BF16), second[...]).astype(BF16)
    node_hidden = silu(dot(gathered, first_weight[...])).astype(BF16)
    normed = layer_norm(dot(node_hidden, node_second[...]), gain[...])
    start = (static[...].astype(F32) + normed).astype(BF16)
    mesh_start[...] = start
    put_table(wide, 0, dot(start, next_source[...]))
    next_table[...] = wide[...].astype(BF16)


def encode(index, strips, own_table, receivers, geometry, edge_weight, weights, static):
    nodes, width = static.shape
    parts = width // LANES
    strip = strips[0].shape[0]
    edges = receivers.shape[1]
    return pl.pallas_call(
        encode_kernel,
        in_specs=[SMEM] + [VMEM] * 6 + [ANY] + [VMEM] * 11,
        out_specs=[VMEM, VMEM],
        out_shape=[
            jax.ShapeDtypeStruct((nodes, width), BF16),
            jax.ShapeDtypeStruct((nodes * parts, LANES), BF16),
        ],
        scratch_shapes=[
            pltpu.VMEM((own_table.shape[0] + 8 * strip * parts, LANES), F32),
            pltpu.VMEM((edges * parts, LANES), F32),
            pltpu.VMEM((nodes, width), F32),
            pltpu.VMEM((nodes * parts, LANES), F32),
            pltpu.SemaphoreType.DMA,
        ],
        compiler_params=params(),
        cost_estimate=cost(2 * edges * width * 2 * width, 10 * 2**20),
    )(
        index, *strips, own_table, receivers, geometry, edge_weight,
        weights[0], weights[1], weights[2], weights[3], weights[4], weights[5], static, weights[6],
    )


def receive_kernel(
    start, target_weight, state_weight, receivers, geometry, edge_weight, shift, state, target
):
    @pl.when(pl.program_id(0) == 0)
    def _():
        target[...] = dot(start[...], target_weight[...]).astype(BF16)
        state[...] = dot(start[...], state_weight[...])

    picks = onehot(receivers[...], start.shape[0])
    shift[...] = (
        dot_rows(picks, target[...]) + dot_rows(geometry[...], edge_weight[...])
    ).astype(BF16)


def receive(start, target_weight, state_weight, receivers, geometry, edge_weight):
    nodes, width = start.shape
    edges = receivers.shape[1]
    tile = 512
    whole = lambda i: (0, 0)
    return pl.pallas_call(
        receive_kernel,
        grid=(edges // tile,),
        in_specs=[
            pl.BlockSpec((nodes, width), whole),
            pl.BlockSpec((width, width), whole),
            pl.BlockSpec((width, width), whole),
            pl.BlockSpec((1, tile), lambda i: (0, i)),
            pl.BlockSpec((geometry.shape[0], tile), lambda i: (0, i)),
            pl.BlockSpec(edge_weight.shape, whole),
        ],
        out_specs=[
            pl.BlockSpec((tile, width), lambda i: (i, 0)),
            pl.BlockSpec((nodes, width), whole),
        ],
        out_shape=[
            jax.ShapeDtypeStruct((edges, width), BF16),
            jax.ShapeDtypeStruct((nodes, width), F32),
        ],
        scratch_shapes=[pltpu.VMEM((nodes, width), BF16)],
        compiler_params=params(),
        cost_estimate=cost(2 * edges * width * 2 * width, 8 * 2**20),
    )(start, target_weight, state_weight, receivers, geometry, edge_weight)


def load_table(blocks, stage, table, sems):
    copies = []
    for slot, (ref, first) in enumerate(blocks):
        count = ref.shape[0]
        copy = pltpu.make_async_copy(ref, stage.at[pl.ds(first, count)], sems.at[slot])
        copy.start()
        copies.append(copy)
    for copy, (ref, first) in zip(copies, blocks):
        copy.wait()
        span = pl.ds(first, ref.shape[0])
        table[span, :] = stage[span, :].astype(F32)


def table_blocks(own, w, e, o, n, oc, ow, oe, nw, ne):
    size = own.shape[0]
    half = size // 2
    blocks = [(ref, slot * size) for slot, ref in enumerate((own, w, e, o, n))]
    blocks += [(oc.at[0], 5 * size), (ow, 5 * size + half)]
    blocks += [(oc.at[1], 6 * size), (oe, 6 * size + half)]
    return blocks + [(nw, 7 * size), (ne, 8 * size)]


def process_kernel(
    index, own, w, e, o, n, oc, ow, oe, nw, ne, receivers, shift, state, start, second,
    message_weight, out_weight, gain, next_source, next_table,
    stage, table, rows, total, wide, sems,
):
    parts = second.shape[0] // LANES
    load_table(table_blocks(own, w, e, o, n, oc, ow, oe, nw, ne), stage, table, sems)
    edges = receivers.shape[1]
    gather(index, 0, edges, table, rows, parts)
    total[...] = jnp.zeros_like(total)
    tile = 512

    def step(i, carry):
        begin = pl.multiple_of(i * tile, tile)
        hidden = [
            silu(
                rows[pl.ds(begin * parts + part, tile, stride=parts), :]
                + shift[pl.ds(begin, tile), part * LANES : (part + 1) * LANES].astype(F32)
            ).astype(BF16)
            for part in range(parts)
        ]
        picks = onehot(receivers[:, pl.ds(begin, tile)], total.shape[0])
        total[...] += dot(picks, jnp.concatenate(hidden, axis=1))
        return carry

    lax.fori_loop(0, edges // tile, step, 0)
    summed = dot(total[...].astype(BF16), second[...]).astype(BF16)
    update = silu(dot(summed, message_weight[...]) + state[...]).astype(BF16)
    normed = layer_norm(dot(update, out_weight[...]), gain[...])
    end = (start[...].astype(F32) + normed).astype(BF16)
    put_table(wide, 0, dot(end, next_source[...]))
    next_table[...] = wide[...].astype(BF16)


def process(index, blocks, receivers, shift, state, start, weights):
    nodes, width = start.shape
    parts = width // LANES
    edges = receivers.shape[1]
    return pl.pallas_call(
        process_kernel,
        in_specs=[SMEM] + [ANY] * 10 + [VMEM] * 9,
        out_specs=VMEM,
        out_shape=jax.ShapeDtypeStruct((nodes * parts, LANES), BF16),
        scratch_shapes=[
            pltpu.VMEM((9 * nodes * parts, LANES), BF16),
            pltpu.VMEM((9 * nodes * parts, LANES), F32),
            pltpu.VMEM((edges * parts, LANES), F32),
            pltpu.VMEM((nodes, width), F32),
            pltpu.VMEM((nodes * parts, LANES), F32),
            pltpu.SemaphoreType.DMA((11,)),
        ],
        compiler_params=params(),
        cost_estimate=cost(2 * edges * width * 2 * width, 12 * 2**20),
    )(index, *blocks, receivers, shift, state, start, *weights)


def decode_kernel(
    index, own, w, e, o, n, oc, ow, oe, nw, ne, embedded, fields, target_weight, hidden_weight,
    output_weight, prediction, stage, table, rows, sems,
):
    tile, width = embedded.shape
    parts = width // LANES
    step = pl.program_id(0)

    @pl.when(step == 0)
    def _():
        load_table(table_blocks(own, w, e, o, n, oc, ow, oe, nw, ne), stage, table, sems)

    senders = 3
    gather(index, step * (senders * tile), senders * tile, table, rows, parts)
    target = dot(embedded[...], target_weight[...])
    summed = []
    for part in range(parts):
        here = target[:, part * LANES : (part + 1) * LANES]
        edge = [
            silu(rows[pl.ds(k * tile * parts + part, tile, stride=parts), :] + here).astype(BF16)
            for k in range(senders)
        ]
        summed.append((edge[0].astype(F32) + edge[1].astype(F32) + edge[2].astype(F32)).astype(BF16))
    final = silu(dot(jnp.concatenate(summed, axis=1), hidden_weight[...])).astype(BF16)
    prediction[...] = fields[...].astype(F32) + dot(final, output_weight[...])


DECODE_TILE = 256


def decode(index, blocks, embedded, fields, target_weight, hidden_weight, output_weight):
    cells, width = embedded.shape
    channels = fields.shape[1]
    parts = width // LANES
    size = blocks[0].shape[0]
    tile = DECODE_TILE
    whole = lambda i: (0, 0)
    return pl.pallas_call(
        decode_kernel,
        grid=(cells // tile,),
        in_specs=[SMEM]
        + [ANY] * 10
        + [
            pl.BlockSpec((tile, width), lambda i: (i, 0)),
            pl.BlockSpec((tile, channels), lambda i: (i, 0)),
            pl.BlockSpec((width, width), whole),
            pl.BlockSpec((width, width), whole),
            pl.BlockSpec((width, channels), whole),
        ],
        out_specs=pl.BlockSpec((tile, channels), lambda i: (i, 0)),
        out_shape=jax.ShapeDtypeStruct((cells, channels), F32),
        scratch_shapes=[
            pltpu.VMEM((9 * size, LANES), BF16),
            pltpu.VMEM((9 * size, LANES), F32),
            pltpu.VMEM((3 * tile * parts, LANES), F32),
            pltpu.SemaphoreType.DMA((11,)),
        ],
        compiler_params=params(),
        cost_estimate=cost(2 * cells * width * 3 * width, 12 * 2**20),
    )(index, *blocks, embedded, fields, target_weight, hidden_weight, output_weight)


def east(values):
    count = lax.axis_size("lon")
    return lax.ppermute(values, "lon", [(i, (i + 1) % count) for i in range(count)])


def west(values):
    count = lax.axis_size("lon")
    return lax.ppermute(values, "lon", [((i + 1) % count, i) for i in range(count)])


def near(values):
    count = lax.axis_size("lat")
    return lax.ppermute(values, "lat", [(i, i ^ 1) for i in range(count)])


def far(values):
    count = lax.axis_size("lat")
    ups = [(i, i + 1) for i in range(1, count - 1, 2)]
    return lax.ppermute(values, "lat", ups + [(b, a) for a, b in ups])


def swap_strips(strip):
    w, e, o, n = east(strip), west(strip), far(strip), near(strip)
    sides = jnp.stack([w, e])
    return w, e, o, n, far(sides), near(sides)


def swap_blocks(block):
    half = block.shape[0] // 2
    w, e, o, n = east(block), west(block), far(block), near(block)
    corners = far(jnp.stack([w[:half], e[:half]]))
    ow, oe = east(o[half:]), west(o[half:])
    return block, w, e, o, n, corners, ow, oe, near(w), near(e)


def slots(block):
    a, b = block // 3, block % 3
    parity = lax.axis_index("lat") % 2
    same = jnp.where(b == 1, 0, jnp.where(b == 0, 1, 2))
    away = jnp.where(b == 1, 3, jnp.where(b == 0, 5, 6))
    close = jnp.where(b == 1, 4, jnp.where(b == 0, 7, 8))
    is_near = (a == 0) == (parity == 1)
    return jnp.where(a == 1, same, jnp.where(is_near, close, away))


def grid_index(senders, cells, strip, parts):
    block, offset = senders // cells, senders % cells
    outside = cells + (slots(block) - 1) * strip + offset % strip
    return jnp.where(block == 4, offset, outside) * parts


def mesh_index(senders, nodes, parts):
    return (slots(senders // nodes) * nodes + senders % nodes) * parts


def split_geometry(geometry, weight):
    def pieces(values):
        high = values.astype(BF16)
        return high, (values - high.astype(F32)).astype(BF16)

    high, low = pieces(geometry)
    weight_high, weight_low = pieces(weight)
    return (
        jnp.concatenate([high, low, high, jnp.zeros_like(high)], axis=0),
        jnp.concatenate(
            [weight_high, weight_high, weight_low, jnp.zeros_like(weight_high)], axis=0
        ),
    )


def valid_receivers(receivers, valid):
    keep = jnp.arange(receivers.shape[0], dtype=jnp.int32) < valid
    return jnp.where(keep, receivers, -1)[None]


def shards(
    grid_fields,
    mesh_static,
    encode_senders,
    encode_receivers,
    encode_geometry,
    encode_valid,
    mesh_senders,
    mesh_receivers,
    mesh_geometry,
    mesh_valid,
    decode_senders,
    embed_weight,
    encode_source,
    encode_edge,
    encode_second,
    node_first,
    node_second,
    node_gain,
    process_source,
    process_target,
    process_edge,
    process_second,
    update_message,
    update_state,
    update_out,
    process_gain,
    decode_source,
    decode_target,
    decode_hidden,
    output_weight,
):
    fields = grid_fields[0, 0]
    static = mesh_static[0, 0]
    cells, nodes, width = fields.shape[0], static.shape[0], static.shape[1]
    parts = width // LANES
    strip = cells // 8
    strips = swap_strips(fields[:strip])
    encode_index = grid_index(encode_senders[0, 0], cells, strip, parts)
    process_index = mesh_index(mesh_senders[0, 0], nodes, parts)
    decode_index = mesh_index(decode_senders[0, 0], nodes, parts)
    decode_index = decode_index.reshape(3, cells // DECODE_TILE, DECODE_TILE)
    decode_index = decode_index.transpose(1, 0, 2).reshape(-1)
    encode_to = valid_receivers(encode_receivers[0, 0], encode_valid[0, 0])
    process_to = valid_receivers(mesh_receivers[0, 0], mesh_valid[0, 0])
    encode_geo, encode_geo_weight = split_geometry(encode_geometry[0, 0], encode_edge)
    process_geo, process_geo_weight = split_geometry(mesh_geometry[0, 0], process_edge)

    embedded, own_table = embed_own(fields, embed_weight, encode_source)
    start, table = encode(
        encode_index,
        strips,
        own_table,
        encode_to,
        encode_geo,
        encode_geo_weight,
        (
            embed_weight,
            encode_source,
            encode_second,
            node_first,
            node_second,
            node_gain[None],
            process_source,
        ),
        static,
    )
    blocks = swap_blocks(table)
    shift, state = receive(
        start, process_target, update_state, process_to, process_geo, process_geo_weight
    )
    table = process(
        process_index,
        blocks,
        process_to,
        shift,
        state,
        start,
        (process_second, update_message, update_out, process_gain[None], decode_source),
    )
    blocks = swap_blocks(table)
    prediction = decode(
        decode_index, blocks, embedded, fields, decode_target, decode_hidden, output_weight
    )
    return prediction[None, None]


def solution(mesh):
    devices = P("lat", "lon")
    in_specs = (devices,) * 11 + (P(),) * 19
    return jax.shard_map(
        shards, mesh=mesh, in_specs=in_specs, out_specs=devices, check_vma=False
    )
```

```python
import functools

import jax
import jax.numpy as jnp
from jax import lax
from jax.experimental import pallas as pl
from jax.experimental.pallas import tpu as pltpu
from jax.sharding import PartitionSpec as P

EPSILON = 1e-05
BF16 = jnp.bfloat16
F32 = jnp.float32
LANES = 128
MIB = 1024 * 1024

VMEM = pl.BlockSpec(memory_space=pltpu.VMEM)
SMEM = pl.BlockSpec(memory_space=pltpu.SMEM)
ANY = pl.BlockSpec(memory_space=pl.ANY)


def params(mib):
    return pltpu.CompilerParams(vmem_limit_bytes=mib * MIB)


def cost(flops, moved):
    return pl.CostEstimate(flops=flops, bytes_accessed=moved, transcendentals=0)


def silu(values):
    half = 0.5 * values
    return half + half * jnp.tanh(half)


def layer_norm(values, gain):
    centre = values - jnp.mean(values, axis=-1, keepdims=True)
    spread = jnp.mean(centre * centre, axis=-1, keepdims=True)
    return centre * lax.rsqrt(spread + EPSILON) * gain


def dot(a, b):
    return jnp.dot(a, b, preferred_element_type=F32)


def dot_rows(a, b):
    return lax.dot_general(a, b, (((0,), (0,)), ((), ())), preferred_element_type=F32)


def put_table(ref, first, values):
    parts = values.shape[1] // LANES
    for part in range(parts):
        ref[pl.ds(first * parts + part, values.shape[0], stride=parts), :] = values[
            :, part * LANES : (part + 1) * LANES
        ]


def gather(index, first, count, table, rows, base, parts):
    for edge in range(count):
        start = pl.multiple_of(index[first + edge], parts)
        rows[pl.ds((base + edge) * parts, parts), :] = table[pl.ds(start, parts), :]


def pipeline(tiles, fetch, work, one, two):
    fetch(0, one, 0, 1)

    def body(pair, carry):
        tile = 2 * pair
        work(tile, one, functools.partial(fetch, tile + 1, two))
        work(tile + 1, two, functools.partial(fetch, jnp.minimum(tile + 2, tiles - 1), one))
        return carry

    lax.fori_loop(0, tiles // 2, body, 0)


def onehot(receivers, begin, valid, nodes):
    shape = receivers.shape
    slot = begin + lax.broadcasted_iota(jnp.int32, shape, 1)
    target = jnp.where(slot < valid, receivers, -1)
    ids = lax.broadcasted_iota(jnp.int32, (nodes, shape[1]), 0)
    return jnp.where(ids == target, 1.0, 0.0).astype(BF16)


def pieces(geometry, order):
    high = geometry.astype(BF16).astype(F32)
    low = geometry - high
    parts = [(high, low)[i] for i in order] + [jnp.zeros_like(high)]
    return jnp.concatenate(parts, axis=0).astype(BF16)


def geometry_term(geometry, edge_weight):
    return dot_rows(pieces(geometry, (0, 1, 0)), pieces(edge_weight, (0, 0, 1)))


def copy_kernel(source, target):
    target[...] = source[...]


def take_strip(fields, strip):
    channels = fields.shape[0]
    block = pl.BlockSpec((channels, strip), lambda i: (0, 0))
    return pl.pallas_call(
        copy_kernel,
        grid=(1,),
        in_specs=[block],
        out_specs=block,
        out_shape=jax.ShapeDtypeStruct((channels, strip), fields.dtype),
        compiler_params=params(60),
        cost_estimate=cost(0, MIB),
    )(fields)


def band_kernel(left, middle, right, band):
    band[...] = jnp.concatenate([left[...], middle[...], right[...]], axis=1)


def make_band(left, middle, right):
    channels, strip = middle.shape
    return pl.pallas_call(
        band_kernel,
        in_specs=[VMEM] * 3,
        out_specs=VMEM,
        out_shape=jax.ShapeDtypeStruct((channels, 3 * strip), middle.dtype),
        compiler_params=params(16),
        cost_estimate=cost(0, MIB),
    )(left, middle, right)


def own_kernel(fields, embed_weight, source_weight, embedded, table):
    values = silu(dot_rows(fields[...], embed_weight[...])).astype(BF16)
    embedded[...] = values
    put_table(table, 0, dot(values, source_weight[...]).astype(BF16).astype(F32))


def embed_own(fields, embed_weight, source_weight):
    channels, cells = fields.shape
    width = embed_weight.shape[1]
    parts = width // LANES
    tile = 512
    return pl.pallas_call(
        own_kernel,
        grid=(cells // tile,),
        in_specs=[
            pl.BlockSpec((channels, tile), lambda i: (0, i)),
            pl.BlockSpec((channels, width), lambda i: (0, 0)),
            pl.BlockSpec((width, width), lambda i: (0, 0)),
        ],
        out_specs=[
            pl.BlockSpec((tile, width), lambda i: (i, 0)),
            pl.BlockSpec((tile * parts, LANES), lambda i: (i, 0)),
        ],
        out_shape=[
            jax.ShapeDtypeStruct((cells, width), BF16),
            jax.ShapeDtypeStruct((cells * parts, LANES), F32),
        ],
        compiler_params=params(20),
        cost_estimate=cost(2 * cells * width * (width + 256), 8 * MIB),
    )(fields, embed_weight, source_weight)


ENCODE_TILE = 512


def encode_kernel(
    index, valid, strip_w, strip_e, strip_far, strip_near, own_table, receivers, geometry,
    edge_weight, embed_weight, source_weight, second, first_weight, node_second, gain, static,
    next_source, mesh_start, next_table, table, one, two, total, wide, sem,
):
    cells = own_table.shape[0]
    parts = second.shape[0] // LANES
    copy = pltpu.make_async_copy(own_table, table.at[pl.ds(0, cells)], sem)
    copy.start()
    done = cells // parts
    sides = jnp.concatenate([strip_w[...], strip_e[...]], axis=1)
    for strip in (sides, strip_far[...], strip_near[...]):
        values = silu(dot_rows(strip, embed_weight[...])).astype(BF16)
        values = dot(values, source_weight[...]).astype(BF16).astype(F32)
        put_table(table, done, values)
        done += strip.shape[1]
    total[...] = jnp.zeros_like(total)
    copy.wait()
    tile = ENCODE_TILE

    def fetch(i, rows, piece, pieces_):
        count = tile // pieces_
        gather(index, i * tile + piece * count, count, table, rows, piece * count, parts)

    def work(i, rows, more):
        begin = pl.multiple_of(i * tile, tile)
        span = pl.ds(begin, tile)
        shift = geometry_term(geometry[:, span], edge_weight[...])
        picks = onehot(receivers[:, span], begin, valid[0, 0], total.shape[0])
        more(0, 8)
        hidden = []
        for part in range(parts):
            here = shift[:, part * LANES : (part + 1) * LANES]
            hidden.append(silu(rows[pl.ds(part, tile, stride=parts), :] + here).astype(BF16))
            more(1 + part, 8)
        more(5, 8)
        total[...] += dot(picks, jnp.concatenate(hidden, axis=1))
        more(6, 8)
        more(7, 8)

    pipeline(receivers.shape[1] // tile, fetch, work, one, two)
    gathered = dot(total[...].astype(BF16), second[...]).astype(BF16)
    node_hidden = silu(dot(gathered, first_weight[...])).astype(BF16)
    normed = layer_norm(dot(node_hidden, node_second[...]), gain[...])
    start = (static[...].astype(F32) + normed).astype(BF16)
    mesh_start[...] = start
    put_table(wide, 0, dot(start, next_source[...]))
    next_table[...] = wide[...].astype(BF16)


def encode(index, valid, strips, own_table, receivers, geometry, edge_weight, weights, static):
    nodes, width = static.shape
    parts = width // LANES
    strip = strips[0].shape[1]
    tile = pltpu.VMEM((ENCODE_TILE * parts, LANES), F32)
    return pl.pallas_call(
        encode_kernel,
        in_specs=[SMEM] * 2 + [VMEM] * 4 + [ANY] + [VMEM] * 11,
        out_specs=[VMEM, VMEM],
        out_shape=[
            jax.ShapeDtypeStruct((nodes, width), BF16),
            jax.ShapeDtypeStruct((nodes * parts, LANES), BF16),
        ],
        scratch_shapes=[
            pltpu.VMEM((own_table.shape[0] + 8 * strip * parts, LANES), F32),
            tile,
            tile,
            pltpu.VMEM((nodes, width), F32),
            pltpu.VMEM((nodes * parts, LANES), F32),
            pltpu.SemaphoreType.DMA,
        ],
        compiler_params=params(36),
        cost_estimate=cost(2 * receivers.shape[1] * width * 2 * width, 10 * MIB),
    )(
        index, valid, *strips, own_table, receivers, geometry, edge_weight,
        weights[0], weights[1], weights[2], weights[3], weights[4], weights[5], static, weights[6],
    )


def receive_kernel(
    valid, start, target_weight, state_weight, receivers, geometry, edge_weight, shift, state, target
):
    @pl.when(pl.program_id(0) == 0)
    def _():
        target[...] = dot(start[...], target_weight[...]).astype(BF16)
        state[...] = dot(start[...], state_weight[...])

    begin = pl.program_id(0) * receivers.shape[1]
    picks = onehot(receivers[...], begin, valid[0, 0], start.shape[0])
    shift[...] = (
        dot_rows(picks, target[...]) + geometry_term(geometry[...], edge_weight[...])
    ).astype(BF16)


def receive(valid, start, target_weight, state_weight, receivers, geometry, edge_weight):
    nodes, width = start.shape
    edges = receivers.shape[1]
    tile = 512
    whole = lambda i: (0, 0)
    return pl.pallas_call(
        receive_kernel,
        grid=(edges // tile,),
        in_specs=[
            SMEM,
            pl.BlockSpec((nodes, width), whole),
            pl.BlockSpec((width, width), whole),
            pl.BlockSpec((width, width), whole),
            pl.BlockSpec((1, tile), lambda i: (0, i)),
            pl.BlockSpec((geometry.shape[0], tile), lambda i: (0, i)),
            pl.BlockSpec(edge_weight.shape, whole),
        ],
        out_specs=[
            pl.BlockSpec((tile, width), lambda i: (i, 0)),
            pl.BlockSpec((nodes, width), whole),
        ],
        out_shape=[
            jax.ShapeDtypeStruct((edges, width), BF16),
            jax.ShapeDtypeStruct((nodes, width), F32),
        ],
        scratch_shapes=[pltpu.VMEM((nodes, width), BF16)],
        compiler_params=params(20),
        cost_estimate=cost(2 * edges * width * 2 * width, 8 * MIB),
    )(valid, start, target_weight, state_weight, receivers, geometry, edge_weight)


def fill_table(blocks, table):
    size = blocks[0].shape[0]
    for slot, block in enumerate(blocks):
        table[pl.ds(slot * size, size), :] = block[...].astype(F32)


PROCESS_TILE = 512


def process_kernel(
    index, valid, b0, b1, b2, b3, b4, b5, b6, b7, b8, receivers, shift, state, start, second,
    message_weight, out_weight, gain, next_source, next_table, table, one, two, total, wide,
):
    parts = second.shape[0] // LANES
    total[...] = jnp.zeros_like(total)
    fill_table((b0, b1, b2, b3, b4, b5, b6, b7, b8), table)
    tile = PROCESS_TILE

    def fetch(i, rows, piece, pieces_):
        count = tile // pieces_
        gather(index, i * tile + piece * count, count, table, rows, piece * count, parts)

    def work(i, rows, more):
        begin = pl.multiple_of(i * tile, tile)
        span = pl.ds(begin, tile)
        picks = onehot(receivers[:, span], begin, valid[0, 0], total.shape[0])
        more(0, 8)
        hidden = []
        for part in range(parts):
            here = shift[span, part * LANES : (part + 1) * LANES].astype(F32)
            hidden.append(silu(rows[pl.ds(part, tile, stride=parts), :] + here).astype(BF16))
            more(1 + part, 8)
        more(5, 8)
        total[...] += dot(picks, jnp.concatenate(hidden, axis=1))
        more(6, 8)
        more(7, 8)

    pipeline(receivers.shape[1] // tile, fetch, work, one, two)
    summed = dot(total[...].astype(BF16), second[...]).astype(BF16)
    update = silu(dot(summed, message_weight[...]) + state[...]).astype(BF16)
    normed = layer_norm(dot(update, out_weight[...]), gain[...])
    end = (start[...].astype(F32) + normed).astype(BF16)
    put_table(wide, 0, dot(end, next_source[...]))
    next_table[...] = wide[...].astype(BF16)


def process(index, valid, blocks, receivers, shift, state, start, weights):
    nodes, width = start.shape
    parts = width // LANES
    edges = receivers.shape[1]
    tile = pltpu.VMEM((PROCESS_TILE * parts, LANES), F32)
    return pl.pallas_call(
        process_kernel,
        in_specs=[SMEM] * 2 + [VMEM] * 18,
        out_specs=VMEM,
        out_shape=jax.ShapeDtypeStruct((nodes * parts, LANES), BF16),
        scratch_shapes=[
            pltpu.VMEM((9 * nodes * parts, LANES), F32),
            tile,
            tile,
            pltpu.VMEM((nodes, width), F32),
            pltpu.VMEM((nodes * parts, LANES), F32),
        ],
        compiler_params=params(36),
        cost_estimate=cost(2 * edges * width * 2 * width, 12 * MIB),
    )(index, valid, *blocks, receivers, shift, state, start, *weights)


DECODE_TILE = 256


def decode_kernel(
    index, b0, b1, b2, b3, b4, b5, b6, b7, b8, embedded, fields, target_weight, hidden_weight,
    output_weight, prediction, table, one, two,
):
    cells, width = embedded.shape
    parts = width // LANES
    fill_table((b0, b1, b2, b3, b4, b5, b6, b7, b8), table)
    tile = DECODE_TILE

    def fetch(i, rows, piece, pieces_):
        count = tile // pieces_
        for k in range(3):
            first = k * cells + i * tile + piece * count
            gather(index, first, count, table, rows, k * tile + piece * count, parts)

    def work(i, rows, more):
        begin = pl.multiple_of(i * tile, tile)
        target = dot(embedded[pl.ds(begin, tile), :], target_weight[...])
        summed = []
        for part in range(parts):
            here = target[:, part * LANES : (part + 1) * LANES]
            edge = [
                silu(rows[pl.ds(k * tile * parts + part, tile, stride=parts), :] + here)
                .astype(BF16)
                .astype(F32)
                for k in range(3)
            ]
            summed.append((edge[0] + edge[1] + edge[2]).astype(BF16))
            more(part, 8)
        more(4, 8)
        more(5, 8)
        final = silu(dot(jnp.concatenate(summed, axis=1), hidden_weight[...])).astype(BF16)
        more(6, 8)
        more(7, 8)
        change = lax.dot_general(
            output_weight[...], final, (((1,), (1,)), ((), ())), preferred_element_type=F32
        )
        result = fields[:, pl.ds(begin, tile)].astype(F32) + change
        prediction[:, 0, pl.ds(begin, tile)] = result

    pipeline(cells // tile, fetch, work, one, two)


def decode(index, blocks, embedded, fields, target_weight, hidden_weight, output_weight):
    cells, width = embedded.shape
    channels = fields.shape[0]
    parts = width // LANES
    size = blocks[0].shape[0]
    tile = pltpu.VMEM((3 * DECODE_TILE * parts, LANES), F32)
    return pl.pallas_call(
        decode_kernel,
        in_specs=[SMEM] + [VMEM] * 14,
        out_specs=VMEM,
        out_shape=jax.ShapeDtypeStruct((channels, 1, cells), F32),
        scratch_shapes=[pltpu.VMEM((9 * size, LANES), F32), tile, tile],
        compiler_params=params(36),
        cost_estimate=cost(2 * cells * width * 3 * width, 12 * MIB),
    )(index, *blocks, embedded, fields, target_weight, hidden_weight, output_weight)


def east(values):
    count = lax.axis_size("lon")
    return lax.ppermute(values, "lon", [(i, (i + 1) % count) for i in range(count)])


def west(values):
    count = lax.axis_size("lon")
    return lax.ppermute(values, "lon", [((i + 1) % count, i) for i in range(count)])


def near(values):
    count = lax.axis_size("lat")
    return lax.ppermute(values, "lat", [(i, i ^ 1) for i in range(count)])


def far(values):
    count = lax.axis_size("lat")
    ups = [(i, i + 1) for i in range(1, count - 1, 2)]
    return lax.ppermute(values, "lat", ups + [(b, a) for a, b in ups])


def swap_strips(strip):
    w, e = east(strip), west(strip)
    band = make_band(w, strip, e)
    return w, e, far(band), near(band)


def lon_shift(values, turn):
    bands, sectors = lax.axis_size("lat"), lax.axis_size("lon")
    pairs = []
    for i in range(bands):
        step = turn if i % 2 == 0 else -turn
        pairs += [(i * sectors + j, i * sectors + (j + step) % sectors) for j in range(sectors)]
    return lax.ppermute(values, ("lat", "lon"), pairs)


def swap_blocks(block):
    fore = lon_shift(block, -1)
    away = far(block)
    close = near(block)
    again, fore = lax.optimization_barrier((block, fore))
    aft = lon_shift(again, 1)
    corner_fore = lon_shift(away, -1)
    corner_aft = far(fore)
    return block, fore, aft, away, close, corner_fore, corner_aft, near(fore), near(aft)


def slots(block, same, away, close):
    a, b = block // 3, block % 3
    is_near = (a == 0) == (lax.axis_index("lat") % 2 == 1)

    def choose(three):
        return jnp.where(b == 0, three[0], jnp.where(b == 1, three[1], three[2]))

    return jnp.where(a == 1, choose(same), jnp.where(is_near, choose(close), choose(away)))


def grid_index(senders, cells, strip, parts):
    block, offset = senders // cells, senders % cells
    slot = slots(block, (0, 0, 1), (2, 3, 4), (5, 6, 7))
    outside = cells + slot * strip + offset % strip
    return jnp.where(block == 4, offset, outside) * parts


def mesh_index(senders, nodes, parts):
    block = senders // nodes
    odd = lax.axis_index("lat") % 2 == 1
    block = jnp.where(odd, block // 3 * 3 + 2 - block % 3, block)
    slot = slots(block, (2, 0, 1), (6, 3, 5), (7, 4, 8))
    return (slot * nodes + senders % nodes) * parts


def shards(
    grid_fields,
    mesh_static,
    encode_senders,
    encode_receivers,
    encode_geometry,
    encode_valid,
    mesh_senders,
    mesh_receivers,
    mesh_geometry,
    mesh_valid,
    decode_senders,
    embed_weight,
    encode_source,
    encode_edge,
    encode_second,
    node_first,
    node_second,
    node_gain,
    process_source,
    process_target,
    process_edge,
    process_second,
    update_message,
    update_state,
    update_out,
    process_gain,
    decode_source,
    decode_target,
    decode_hidden,
    output_weight,
):
    fields = grid_fields[0, 0].T
    static = mesh_static[0, 0]
    cells, nodes, width = fields.shape[1], static.shape[0], static.shape[1]
    parts = width // LANES
    strip = cells // 8
    strips = swap_strips(take_strip(fields, strip))
    encode_index = grid_index(encode_senders[0, 0], cells, strip, parts)
    process_index = mesh_index(mesh_senders[0, 0], nodes, parts)
    decode_index = mesh_index(decode_senders[0, 0].reshape(-1), nodes, parts)
    embedded, own_table = embed_own(fields, embed_weight, encode_source)
    start, table = encode(
        encode_index,
        encode_valid,
        strips,
        own_table,
        encode_receivers[0],
        encode_geometry[0, 0],
        encode_edge,
        (
            embed_weight,
            encode_source,
            encode_second,
            node_first,
            node_second,
            node_gain[None],
            process_source,
        ),
        static,
    )
    blocks = swap_blocks(table)
    shift, state = receive(
        mesh_valid,
        start,
        process_target,
        update_state,
        mesh_receivers[0],
        mesh_geometry[0, 0],
        process_edge,
    )
    table = process(
        process_index,
        mesh_valid,
        blocks,
        mesh_receivers[0],
        shift,
        state,
        start,
        (process_second, update_message, update_out, process_gain[None], decode_source),
    )
    blocks = swap_blocks(table)
    prediction = decode(
        decode_index, blocks, embedded, fields, decode_target, decode_hidden, output_weight.T
    )
    return prediction.transpose(1, 2, 0)[None]


def solution(mesh):
    devices = P("lat", "lon")
    in_specs = (devices,) * 11 + (P(),) * 19
    return jax.shard_map(
        shards, mesh=mesh, in_specs=in_specs, out_specs=devices, check_vma=False
    )
```

```python
import functools

import jax
import jax.numpy as jnp
from jax import lax
from jax.experimental import pallas as pl
from jax.experimental.pallas import tpu as pltpu
from jax.sharding import PartitionSpec as P

EPSILON = 1e-05
BF16 = jnp.bfloat16
F32 = jnp.float32
LANES = 128
MIB = 1024 * 1024

VMEM = pl.BlockSpec(memory_space=pltpu.VMEM)
SMEM = pl.BlockSpec(memory_space=pltpu.SMEM)
ANY = pl.BlockSpec(memory_space=pl.ANY)
HBM = pl.BlockSpec(memory_space=pltpu.HBM)


def params(mib):
    return pltpu.CompilerParams(vmem_limit_bytes=mib * MIB)


def cost(flops, moved):
    return pl.CostEstimate(flops=flops, bytes_accessed=moved, transcendentals=0)


def silu(values):
    half = 0.5 * values
    return half + half * jnp.tanh(half)


def silu_half(values):
    half = (0.5 * values).astype(BF16)
    return half + half * jnp.tanh(half)


def layer_norm(values, gain):
    centre = values - jnp.mean(values, axis=-1, keepdims=True)
    spread = jnp.mean(centre * centre, axis=-1, keepdims=True)
    return centre * lax.rsqrt(spread + EPSILON) * gain


def dot(a, b):
    return jnp.dot(a, b, preferred_element_type=F32)


def dot_rows(a, b):
    return lax.dot_general(a, b, (((0,), (0,)), ((), ())), preferred_element_type=F32)


def put_table(ref, first, values):
    parts = values.shape[1] // LANES
    for part in range(parts):
        ref[pl.ds(first * parts + part, values.shape[0], stride=parts), :] = values[
            :, part * LANES : (part + 1) * LANES
        ]


def gather(index, first, count, table, rows, base, parts):
    for edge in range(count):
        start = pl.multiple_of(index[first + edge], parts)
        rows[pl.ds((base + edge) * parts, parts), :] = table[pl.ds(start, parts), :]


def pipeline(tiles, fetch, work, one, two, at_pair=lambda pair: None):
    fetch(0, one, 0, 1)

    def body(pair, carry):
        at_pair(pair)
        tile = 2 * pair
        work(tile, one, functools.partial(fetch, tile + 1, two))
        work(tile + 1, two, functools.partial(fetch, jnp.minimum(tile + 2, tiles - 1), one))
        return carry

    lax.fori_loop(0, tiles // 2, body, 0)


def onehot(receivers, begin, valid, nodes):
    shape = receivers.shape
    slot = begin + lax.broadcasted_iota(jnp.int32, shape, 1)
    target = jnp.where(slot < valid, receivers, -1)
    ids = lax.broadcasted_iota(jnp.int32, (nodes, shape[1]), 0)
    return jnp.where(ids == target, 1.0, 0.0).astype(BF16)


def pieces(geometry, order):
    high = geometry.astype(BF16).astype(F32)
    low = geometry - high
    parts = [(high, low)[i] for i in order] + [jnp.zeros_like(high)]
    return jnp.concatenate(parts, axis=0).astype(BF16)


def geometry_term(geometry, edge_weight):
    return dot_rows(pieces(geometry, (0, 1, 0)), pieces(edge_weight, (0, 0, 1)))


def strip_kernel(fields, kept, strip, sem):
    copy = pltpu.make_async_copy(fields.at[:, pl.ds(0, strip.shape[1])], strip, sem)
    copy.start()
    copy.wait()


def take_strip(fields, strip):
    channels = fields.shape[0]
    return pl.pallas_call(
        strip_kernel,
        in_specs=[ANY],
        out_specs=[ANY, VMEM],
        out_shape=[
            jax.ShapeDtypeStruct(fields.shape, fields.dtype),
            jax.ShapeDtypeStruct((channels, strip), fields.dtype),
        ],
        scratch_shapes=[pltpu.SemaphoreType.DMA],
        input_output_aliases={0: 0},
        compiler_params=params(16),
        cost_estimate=cost(0, MIB),
    )(fields)


def band_kernel(left, middle, right, band):
    band[...] = jnp.concatenate([left[...], middle[...], right[...]], axis=1)


def make_band(left, middle, right):
    channels, strip = middle.shape
    return pl.pallas_call(
        band_kernel,
        in_specs=[VMEM] * 3,
        out_specs=VMEM,
        out_shape=jax.ShapeDtypeStruct((channels, 3 * strip), middle.dtype),
        compiler_params=params(16),
        cost_estimate=cost(4 * 10**9, MIB),
    )(left, middle, right)


OWN_TILE = 512


def own_kernel(
    fields_hbm, embed_hbm, source_hbm, embedded, table, fields, embed_weight, source_weight, sems
):
    cells, width = embedded.shape
    tile = OWN_TILE
    weights = [
        pltpu.make_async_copy(embed_hbm, embed_weight, sems.at[0]),
        pltpu.make_async_copy(source_hbm, source_weight, sems.at[1]),
    ]
    weights[0].start()
    loads = []
    for i in range(cells // tile):
        span = pl.ds(i * tile, tile)
        loads.append(pltpu.make_async_copy(fields_hbm.at[:, span], fields.at[:, span], sems.at[2 + i]))
        loads[-1].start()
    weights[1].start()
    weights[0].wait()
    for i in range(cells // tile):
        span = pl.ds(i * tile, tile)
        loads[i].wait()
        values = silu(dot_rows(fields[:, span], embed_weight[...])).astype(BF16)
        embedded[span, :] = values
        if i == 0:
            weights[1].wait()
        put_table(table, i * tile, dot(values, source_weight[...]))


def embed_own(fields, embed_weight, source_weight):
    channels, cells = fields.shape
    width = embed_weight.shape[1]
    parts = width // LANES
    return pl.pallas_call(
        own_kernel,
        in_specs=[ANY] * 3,
        out_specs=[VMEM, VMEM],
        out_shape=[
            jax.ShapeDtypeStruct((cells, width), BF16),
            jax.ShapeDtypeStruct((cells * parts, LANES), F32),
        ],
        scratch_shapes=[
            pltpu.VMEM(fields.shape, BF16),
            pltpu.VMEM(embed_weight.shape, BF16),
            pltpu.VMEM(source_weight.shape, BF16),
            pltpu.SemaphoreType.DMA((2 + cells // OWN_TILE,)),
        ],
        compiler_params=params(20),
        cost_estimate=cost(2 * cells * width * (width + 256), 8 * MIB),
    )(fields, embed_weight, source_weight)


ENCODE_TILE = 512


def encode_kernel(
    index, valid, strip_w, strip_e, strip_far, strip_near, own_table, receivers, geometry,
    edge_weight, embed_weight, source_weight, second, first_weight, node_second, gain, static,
    next_source, mesh_start, next_table, table, one, two, total, wide, sem,
):
    cells = own_table.shape[0]
    parts = second.shape[0] // LANES
    copy = pltpu.make_async_copy(own_table, table.at[pl.ds(0, cells)], sem)
    copy.start()
    done = cells // parts
    sides = jnp.concatenate([strip_w[...], strip_e[...]], axis=1)
    for strip in (sides, strip_far[...], strip_near[...]):
        values = silu_half(dot_rows(strip, embed_weight[...]))
        put_table(table, done, dot(values, source_weight[...]))
        done += strip.shape[1]
    total[...] = jnp.zeros_like(total)
    copy.wait()
    tile = ENCODE_TILE

    def fetch(i, rows, piece, pieces_):
        count = tile // pieces_
        gather(index, i * tile + piece * count, count, table, rows, piece * count, parts)

    def work(i, rows, more):
        begin = pl.multiple_of(i * tile, tile)
        span = pl.ds(begin, tile)
        shift = geometry_term(geometry[:, span], edge_weight[...])
        picks = onehot(receivers[:, span], begin, valid[0, 0], total.shape[0])
        more(0, 8)
        hidden = []
        for part in range(parts):
            here = shift[:, part * LANES : (part + 1) * LANES]
            hidden.append(silu_half(rows[pl.ds(part, tile, stride=parts), :] + here))
            more(1 + part, 8)
        more(5, 8)
        total[...] += dot(picks, jnp.concatenate(hidden, axis=1))
        more(6, 8)
        more(7, 8)

    pipeline(receivers.shape[1] // tile, fetch, work, one, two)
    gathered = dot(total[...].astype(BF16), second[...]).astype(BF16)
    node_hidden = silu(dot(gathered, first_weight[...])).astype(BF16)
    normed = layer_norm(dot(node_hidden, node_second[...]), gain[...])
    start = (static[...].astype(F32) + normed).astype(BF16)
    mesh_start[...] = start
    put_table(wide, 0, dot(start, next_source[...]))
    next_table[...] = wide[...].astype(BF16)


def encode(index, valid, strips, own_table, receivers, geometry, edge_weight, weights, static):
    nodes, width = static.shape
    parts = width // LANES
    strip = strips[0].shape[1]
    tile = pltpu.VMEM((ENCODE_TILE * parts, LANES), F32)
    return pl.pallas_call(
        encode_kernel,
        in_specs=[SMEM] * 2 + [VMEM] * 4 + [ANY] + [VMEM] * 11,
        out_specs=[VMEM, VMEM],
        out_shape=[
            jax.ShapeDtypeStruct((nodes, width), BF16),
            jax.ShapeDtypeStruct((nodes * parts, LANES), BF16),
        ],
        scratch_shapes=[
            pltpu.VMEM((own_table.shape[0] + 8 * strip * parts, LANES), F32),
            tile,
            tile,
            pltpu.VMEM((nodes, width), F32),
            pltpu.VMEM((nodes * parts, LANES), F32),
            pltpu.SemaphoreType.DMA,
        ],
        compiler_params=params(36),
        cost_estimate=cost(2 * receivers.shape[1] * width * 2 * width, 10 * MIB),
    )(
        index, valid, *strips, own_table, receivers, geometry, edge_weight,
        weights[0], weights[1], weights[2], weights[3], weights[4], weights[5], static, weights[6],
    )


def edge_shift(receivers, geometry, edge_weight, target):
    ids = lax.broadcasted_iota(jnp.int32, (target.shape[0], receivers.shape[1]), 0)
    picks = jnp.where(ids == receivers, 1.0, 0.0).astype(BF16)
    return (dot_rows(picks, target) + geometry_term(geometry, edge_weight)).astype(BF16)


def receive_kernel(
    start, target_weight, state_weight, receivers, geometry, edge_weight, shift, state, target
):
    @pl.when(pl.program_id(0) == 0)
    def _():
        target[...] = dot(start[...], target_weight[...]).astype(BF16)
        state[...] = dot(start[...], state_weight[...])

    shift[...] = edge_shift(receivers[...], geometry[...], edge_weight[...], target[...])


def receive_rest_kernel(target, receivers, geometry, edge_weight, shift_before, shift):
    shift[...] = edge_shift(receivers[...], geometry[...], edge_weight[...], target[...])


RECEIVE_TILE = 512


def whole(i):
    return 0, 0


def receive(start, target_weight, state_weight, receivers, geometry, edge_weight, tiles):
    nodes, width = start.shape
    edges = receivers.shape[1]
    tile = RECEIVE_TILE
    square = pl.BlockSpec((width, width), whole)
    return pl.pallas_call(
        receive_kernel,
        grid=(tiles,),
        in_specs=[
            pl.BlockSpec((nodes, width), whole),
            square,
            square,
            pl.BlockSpec((1, tile), lambda i: (0, i)),
            pl.BlockSpec((geometry.shape[0], tile), lambda i: (0, i)),
            pl.BlockSpec(edge_weight.shape, whole),
        ],
        out_specs=[
            pl.BlockSpec((tile, width), lambda i: (i, 0)),
            pl.BlockSpec((nodes, width), whole),
            pl.BlockSpec((nodes, width), whole),
        ],
        out_shape=[
            jax.ShapeDtypeStruct((edges, width), BF16),
            jax.ShapeDtypeStruct((nodes, width), F32),
            jax.ShapeDtypeStruct((nodes, width), BF16),
        ],
        compiler_params=params(20),
        cost_estimate=cost(2 * tiles * tile * width * 2 * width, 8 * MIB),
    )(start, target_weight, state_weight, receivers, geometry, edge_weight)


def receive_rest(target, receivers, geometry, edge_weight, shift, tiles):
    nodes, width = target.shape
    tile = RECEIVE_TILE
    rest = receivers.shape[1] // tile - tiles
    return pl.pallas_call(
        receive_rest_kernel,
        grid=(rest,),
        in_specs=[
            pl.BlockSpec((nodes, width), whole),
            pl.BlockSpec((1, tile), lambda i: (0, i + tiles)),
            pl.BlockSpec((geometry.shape[0], tile), lambda i: (0, i + tiles)),
            pl.BlockSpec(edge_weight.shape, whole),
            ANY,
        ],
        out_specs=pl.BlockSpec((tile, width), lambda i: (i + tiles, 0)),
        out_shape=jax.ShapeDtypeStruct(shift.shape, BF16),
        input_output_aliases={4: 0},
        compiler_params=params(20),
        cost_estimate=cost(2 * rest * tile * width * 2 * width, 8 * MIB),
    )(target, receivers, geometry, edge_weight, shift)


def fill_table(blocks, table):
    size = blocks[0].shape[0]
    for slot, block in enumerate(blocks):
        table[pl.ds(slot * size, size), :] = block[...].astype(F32)


PROCESS_TILE = 512


def process_kernel(
    index, valid, b0, b1, b2, b3, b4, b5, b6, b7, b8, receivers, shift, state, start, second,
    message_weight, out_weight, gain, next_source, next_table, table, one, two, total, wide,
):
    parts = second.shape[0] // LANES
    total[...] = jnp.zeros_like(total)
    fill_table((b0, b1, b2, b3, b4, b5, b6, b7, b8), table)
    tile = PROCESS_TILE

    def fetch(i, rows, piece, pieces_):
        count = tile // pieces_
        gather(index, i * tile + piece * count, count, table, rows, piece * count, parts)

    def work(i, rows, more):
        begin = pl.multiple_of(i * tile, tile)
        span = pl.ds(begin, tile)
        picks = onehot(receivers[:, span], begin, valid[0, 0], total.shape[0])
        more(0, 8)
        hidden = []
        for part in range(parts):
            here = shift[span, part * LANES : (part + 1) * LANES].astype(F32)
            hidden.append(silu_half(rows[pl.ds(part, tile, stride=parts), :] + here))
            more(1 + part, 8)
        more(5, 8)
        total[...] += dot(picks, jnp.concatenate(hidden, axis=1))
        more(6, 8)
        more(7, 8)

    pipeline(receivers.shape[1] // tile, fetch, work, one, two)
    summed = dot(total[...].astype(BF16), second[...]).astype(BF16)
    update = silu(dot(summed, message_weight[...]) + state[...]).astype(BF16)
    normed = layer_norm(dot(update, out_weight[...]), gain[...])
    end = (start[...].astype(F32) + normed).astype(BF16)
    put_table(wide, 0, dot(end, next_source[...]))
    next_table[...] = wide[...].astype(BF16)


def process(index, valid, blocks, receivers, shift, state, start, weights):
    nodes, width = start.shape
    parts = width // LANES
    edges = receivers.shape[1]
    tile = pltpu.VMEM((PROCESS_TILE * parts, LANES), F32)
    return pl.pallas_call(
        process_kernel,
        in_specs=[SMEM] * 2 + [VMEM] * 18,
        out_specs=VMEM,
        out_shape=jax.ShapeDtypeStruct((nodes * parts, LANES), BF16),
        scratch_shapes=[
            pltpu.VMEM((9 * nodes * parts, LANES), F32),
            tile,
            tile,
            pltpu.VMEM((nodes, width), F32),
            pltpu.VMEM((nodes * parts, LANES), F32),
        ],
        compiler_params=params(36),
        cost_estimate=cost(2 * edges * width * 2 * width, 12 * MIB),
    )(index, valid, *blocks, receivers, shift, state, start, *weights)


def target_kernel(embedded, weight, target):
    target[...] = dot(embedded[...], weight[...]).astype(BF16)


def grid_target(embedded, weight):
    cells, width = embedded.shape
    tile = 512
    return pl.pallas_call(
        target_kernel,
        grid=(cells // tile,),
        in_specs=[
            pl.BlockSpec((tile, width), lambda i: (i, 0)),
            pl.BlockSpec((width, width), lambda i: (0, 0)),
        ],
        out_specs=pl.BlockSpec((tile, width), lambda i: (i, 0)),
        out_shape=jax.ShapeDtypeStruct((cells, width), BF16),
        compiler_params=params(16),
        cost_estimate=cost(2 * cells * width * width, 4 * MIB),
    )(embedded, weight)


DECODE_TILE = 512


def decode_kernel(
    index, b0, b1, b2, b3, b4, b5, b6, b7, b8, target, fields, hidden_weight, output_weight,
    prediction, table, one, two, result, sems,
):
    cells, width = target.shape
    parts = width // LANES
    fill_table((b0, b1, b2, b3, b4, b5, b6, b7, b8), table)
    tile = DECODE_TILE
    tiles = cells // tile
    halves = [
        pltpu.make_async_copy(result.at[:, :, span], prediction.at[:, :, span], sems.at[i])
        for i, span in enumerate((pl.ds(0, cells // 2), pl.ds(cells // 2, cells // 2)))
    ]

    def fetch(i, rows, piece, pieces_):
        count = tile // pieces_
        for k in range(3):
            first = k * cells + i * tile + piece * count
            gather(index, first, count, table, rows, k * tile + piece * count, parts)

    def work(i, rows, more):
        begin = pl.multiple_of(i * tile, tile)
        span = pl.ds(begin, tile)
        summed = []
        for part in range(parts):
            here = target[span, part * LANES : (part + 1) * LANES].astype(F32)
            edge = [
                silu_half(rows[pl.ds(k * tile * parts + part, tile, stride=parts), :] + here)
                for k in range(3)
            ]
            total = edge[0].astype(F32) + edge[1].astype(F32) + edge[2].astype(F32)
            summed.append(total.astype(BF16))
            more(part, 8)
        more(4, 8)
        more(5, 8)
        final = silu_half(dot(jnp.concatenate(summed, axis=1), hidden_weight[...]))
        more(6, 8)
        more(7, 8)
        change = lax.dot_general(
            output_weight[...], final, (((1,), (1,)), ((), ())), preferred_element_type=F32
        )
        result[:, 0, span] = fields[:, span].astype(F32) + change

    def at_pair(pair):
        @pl.when(pair == tiles // 4)
        def _():
            halves[0].start()

    pipeline(tiles, fetch, work, one, two, at_pair)
    halves[1].start()
    halves[0].wait()
    halves[1].wait()


def decode(index, blocks, target, fields, hidden_weight, output_weight):
    cells, width = target.shape
    channels = fields.shape[0]
    parts = width // LANES
    size = blocks[0].shape[0]
    tile = pltpu.VMEM((3 * DECODE_TILE * parts, LANES), F32)
    return pl.pallas_call(
        decode_kernel,
        in_specs=[SMEM] + [VMEM] * 13,
        out_specs=HBM,
        out_shape=jax.ShapeDtypeStruct((channels, 1, cells), F32),
        scratch_shapes=[
            pltpu.VMEM((9 * size, LANES), F32),
            tile,
            tile,
            pltpu.VMEM((channels, 1, cells), F32),
            pltpu.SemaphoreType.DMA((2,)),
        ],
        compiler_params=params(36),
        cost_estimate=cost(2 * cells * width * 3 * width, 12 * MIB),
    )(index, *blocks, target, fields, hidden_weight, output_weight)


def east(values):
    count = lax.axis_size("lon")
    return lax.ppermute(values, "lon", [(i, (i + 1) % count) for i in range(count)])


def west(values):
    count = lax.axis_size("lon")
    return lax.ppermute(values, "lon", [((i + 1) % count, i) for i in range(count)])


def near(values):
    count = lax.axis_size("lat")
    return lax.ppermute(values, "lat", [(i, i ^ 1) for i in range(count)])


def far(values):
    count = lax.axis_size("lat")
    ups = [(i, i + 1) for i in range(1, count - 1, 2)]
    return lax.ppermute(values, "lat", ups + [(b, a) for a, b in ups])


def swap_strips(strip):
    w, e = east(strip), west(strip)
    band = make_band(w, strip, e)
    return w, e, far(band), near(band)


def lon_shift(values, turn):
    bands, sectors = lax.axis_size("lat"), lax.axis_size("lon")
    pairs = []
    for i in range(bands):
        step = turn if i % 2 == 0 else -turn
        pairs += [(i * sectors + j, i * sectors + (j + step) % sectors) for j in range(sectors)]
    return lax.ppermute(values, ("lat", "lon"), pairs)


def swap_blocks(block, beside=tuple):
    fore = lon_shift(block, -1)
    away = far(block)
    close = near(block)
    again, fore, work = lax.optimization_barrier((block, fore, beside()))
    aft = lon_shift(again, 1)
    corner_fore = lon_shift(away, -1)
    corner_aft = far(fore)
    blocks = block, fore, aft, away, close, corner_fore, corner_aft, near(fore), near(aft)
    return blocks, work


def slots(block, same, away, close):
    a, b = block // 3, block % 3
    is_near = (a == 0) == (lax.axis_index("lat") % 2 == 1)

    def choose(three):
        return jnp.where(b == 0, three[0], jnp.where(b == 1, three[1], three[2]))

    return jnp.where(a == 1, choose(same), jnp.where(is_near, choose(close), choose(away)))


def grid_index(senders, cells, strip, parts):
    block, offset = senders // cells, senders % cells
    slot = slots(block, (0, 0, 1), (2, 3, 4), (5, 6, 7))
    outside = cells + slot * strip + offset % strip
    return jnp.where(block == 4, offset, outside) * parts


def mesh_index(senders, nodes, parts):
    block = senders // nodes
    odd = lax.axis_index("lat") % 2 == 1
    block = jnp.where(odd, block // 3 * 3 + 2 - block % 3, block)
    slot = slots(block, (2, 0, 1), (6, 3, 5), (7, 4, 8))
    return (slot * nodes + senders % nodes) * parts


def shards(
    grid_fields,
    mesh_static,
    encode_senders,
    encode_receivers,
    encode_geometry,
    encode_valid,
    mesh_senders,
    mesh_receivers,
    mesh_geometry,
    mesh_valid,
    decode_senders,
    embed_weight,
    encode_source,
    encode_edge,
    encode_second,
    node_first,
    node_second,
    node_gain,
    process_source,
    process_target,
    process_edge,
    process_second,
    update_message,
    update_state,
    update_out,
    process_gain,
    decode_source,
    decode_target,
    decode_hidden,
    output_weight,
):
    fields = grid_fields[0, 0].T
    static = mesh_static[0, 0]
    cells, nodes, width = fields.shape[1], static.shape[0], static.shape[1]
    parts = width // LANES
    strip = cells // 8
    fields, own_strip = take_strip(fields, strip)
    strips = swap_strips(own_strip)
    encode_index = grid_index(encode_senders[0, 0], cells, strip, parts)
    process_index = mesh_index(mesh_senders[0, 0], nodes, parts)
    decode_index = mesh_index(decode_senders[0, 0].reshape(-1), nodes, parts)
    embedded, own_table = embed_own(fields, embed_weight, encode_source)
    start, table = encode(
        encode_index,
        encode_valid,
        strips,
        own_table,
        encode_receivers[0],
        encode_geometry[0, 0],
        encode_edge,
        (
            embed_weight,
            encode_source,
            encode_second,
            node_first,
            node_second,
            node_gain[None],
            process_source,
        ),
        static,
    )
    receivers, geometry = mesh_receivers[0], mesh_geometry[0, 0]
    tiles = receivers.shape[1] // RECEIVE_TILE * 5 // 8
    blocks, (shift, state, target) = swap_blocks(
        table,
        lambda: receive(
            start, process_target, update_state, receivers, geometry, process_edge, tiles
        ),
    )
    shift = receive_rest(target, receivers, geometry, process_edge, shift, tiles)
    table = process(
        process_index,
        mesh_valid,
        blocks,
        receivers,
        shift,
        state,
        start,
        (process_second, update_message, update_out, process_gain[None], decode_source),
    )
    blocks, _ = swap_blocks(table)
    target = grid_target(embedded, decode_target)
    prediction = decode(decode_index, blocks, target, fields, decode_hidden, output_weight.T)
    return prediction.transpose(1, 2, 0)[None]


def solution(mesh):
    devices = P("lat", "lon")
    in_specs = (devices,) * 11 + (P(),) * 19
    return jax.shard_map(
        shards, mesh=mesh, in_specs=in_specs, out_specs=devices, check_vma=False
    )
```

```python
import functools

import jax
import jax.numpy as jnp
from jax import lax
from jax.experimental import pallas as pl
from jax.experimental.pallas import tpu as pltpu
from jax.sharding import PartitionSpec as P

EPSILON = 1e-05
BF16 = jnp.bfloat16
F32 = jnp.float32
LANES = 128
MIB = 1024 * 1024

VMEM = pl.BlockSpec(memory_space=pltpu.VMEM)
SMEM = pl.BlockSpec(memory_space=pltpu.SMEM)
ANY = pl.BlockSpec(memory_space=pl.ANY)
HBM = pl.BlockSpec(memory_space=pltpu.HBM)


def params(mib):
    return pltpu.CompilerParams(vmem_limit_bytes=mib * MIB)


def cost(flops, moved):
    return pl.CostEstimate(flops=flops, bytes_accessed=moved, transcendentals=0)


def silu(values):
    half = 0.5 * values
    return half + half * jnp.tanh(half)


def silu_half(values):
    half = (0.5 * values).astype(BF16)
    return half + half * jnp.tanh(half)


def layer_norm(values, gain):
    centre = values - jnp.mean(values, axis=-1, keepdims=True)
    spread = jnp.mean(centre * centre, axis=-1, keepdims=True)
    return centre * lax.rsqrt(spread + EPSILON) * gain


def dot(a, b):
    return jnp.dot(a, b, preferred_element_type=F32)


def dot_rows(a, b):
    return lax.dot_general(a, b, (((0,), (0,)), ((), ())), preferred_element_type=F32)


def put_table(ref, first, values):
    parts = values.shape[1] // LANES
    for part in range(parts):
        ref[pl.ds(first * parts + part, values.shape[0], stride=parts), :] = values[
            :, part * LANES : (part + 1) * LANES
        ]


def gather(index, first, count, table, rows, base, parts):
    for edge in range(count):
        start = pl.multiple_of(index[first + edge], parts)
        rows[pl.ds((base + edge) * parts, parts), :] = table[pl.ds(start, parts), :]


def pipeline(tiles, fetch, work, one, two, at_pair=lambda pair: None):
    fetch(0, one, 0, 1)

    def nothing(piece, pieces_):
        pass

    def body(pair, carry):
        at_pair(pair)
        tile = 2 * pair
        work(tile, one, functools.partial(fetch, tile + 1, two))
        work(tile + 1, two, functools.partial(fetch, tile + 2, one))
        return carry

    lax.fori_loop(0, tiles // 2 - 1, body, 0)
    at_pair(tiles // 2 - 1)
    work(tiles - 2, one, functools.partial(fetch, tiles - 1, two))
    work(tiles - 1, two, nothing)


def onehot(receivers, begin, valid, nodes):
    shape = receivers.shape
    slot = begin + lax.broadcasted_iota(jnp.int32, shape, 1)
    target = jnp.where(slot < valid, receivers, -1)
    ids = lax.broadcasted_iota(jnp.int32, (nodes, shape[1]), 0)
    return jnp.where(ids == target, 1.0, 0.0).astype(BF16)


def pieces(geometry, order):
    high = geometry.astype(BF16).astype(F32)
    low = geometry - high
    parts = [(high, low)[i] for i in order] + [jnp.zeros_like(high)]
    return jnp.concatenate(parts, axis=0).astype(BF16)


def geometry_term(geometry, edge_weight):
    return dot_rows(pieces(geometry, (0, 1, 0)), pieces(edge_weight, (0, 0, 1)))


def strip_kernel(fields, kept, strip, sem):
    copy = pltpu.make_async_copy(fields.at[:, pl.ds(0, strip.shape[1])], strip, sem)
    copy.start()
    copy.wait()


def take_strip(fields, strip):
    channels = fields.shape[0]
    return pl.pallas_call(
        strip_kernel,
        in_specs=[ANY],
        out_specs=[ANY, VMEM],
        out_shape=[
            jax.ShapeDtypeStruct(fields.shape, fields.dtype),
            jax.ShapeDtypeStruct((channels, strip), fields.dtype),
        ],
        scratch_shapes=[pltpu.SemaphoreType.DMA],
        input_output_aliases={0: 0},
        compiler_params=params(16),
        cost_estimate=cost(0, MIB),
    )(fields)


def band_kernel(left, middle, right, band):
    band[...] = jnp.concatenate([left[...], middle[...], right[...]], axis=1)


def make_band(left, middle, right):
    channels, strip = middle.shape
    return pl.pallas_call(
        band_kernel,
        in_specs=[VMEM] * 3,
        out_specs=VMEM,
        out_shape=jax.ShapeDtypeStruct((channels, 3 * strip), middle.dtype),
        compiler_params=params(16),
        cost_estimate=cost(4 * 10**9, MIB),
    )(left, middle, right)


OWN_TILE = 512


def own_kernel(
    fields_hbm, embed_hbm, source_hbm, embedded, table, fields, embed_weight, source_weight, sems
):
    cells, width = embedded.shape
    tile = OWN_TILE
    weights = [
        pltpu.make_async_copy(embed_hbm, embed_weight, sems.at[0]),
        pltpu.make_async_copy(source_hbm, source_weight, sems.at[1]),
    ]
    weights[0].start()
    loads = []
    for i in range(cells // tile):
        span = pl.ds(i * tile, tile)
        loads.append(pltpu.make_async_copy(fields_hbm.at[:, span], fields.at[:, span], sems.at[2 + i]))
        loads[-1].start()
    weights[1].start()
    weights[0].wait()
    for i in range(cells // tile):
        span = pl.ds(i * tile, tile)
        loads[i].wait()
        values = silu(dot_rows(fields[:, span], embed_weight[...])).astype(BF16)
        embedded[span, :] = values
        if i == 0:
            weights[1].wait()
        put_table(table, i * tile, dot(values, source_weight[...]))


def embed_own(fields, embed_weight, source_weight):
    channels, cells = fields.shape
    width = embed_weight.shape[1]
    parts = width // LANES
    return pl.pallas_call(
        own_kernel,
        in_specs=[ANY] * 3,
        out_specs=[VMEM, VMEM],
        out_shape=[
            jax.ShapeDtypeStruct((cells, width), BF16),
            jax.ShapeDtypeStruct((cells * parts, LANES), F32),
        ],
        scratch_shapes=[
            pltpu.VMEM(fields.shape, BF16),
            pltpu.VMEM(embed_weight.shape, BF16),
            pltpu.VMEM(source_weight.shape, BF16),
            pltpu.SemaphoreType.DMA((2 + cells // OWN_TILE,)),
        ],
        compiler_params=params(20),
        cost_estimate=cost(2 * cells * width * (width + 256), 8 * MIB),
    )(fields, embed_weight, source_weight)


ENCODE_TILE = 512


def encode_kernel(
    index, valid, strip_w, strip_e, strip_far, strip_near, own_table, receivers, geometry,
    edge_weight, embed_weight, source_weight, second, first_weight, node_second, gain, static,
    next_source, mesh_start, next_table, table, one, two, total, wide, sem,
):
    cells = own_table.shape[0]
    parts = second.shape[0] // LANES
    copy = pltpu.make_async_copy(own_table, table.at[pl.ds(0, cells)], sem)
    copy.start()
    done = cells // parts
    sides = jnp.concatenate([strip_w[...], strip_e[...]], axis=1)
    for strip in (sides, strip_far[...], strip_near[...]):
        values = silu_half(dot_rows(strip, embed_weight[...]))
        put_table(table, done, dot(values, source_weight[...]))
        done += strip.shape[1]
    total[...] = jnp.zeros_like(total)
    copy.wait()
    tile = ENCODE_TILE

    def fetch(i, rows, piece, pieces_):
        count = tile // pieces_
        gather(index, i * tile + piece * count, count, table, rows, piece * count, parts)

    def work(i, rows, more):
        begin = pl.multiple_of(i * tile, tile)
        span = pl.ds(begin, tile)
        shift = geometry_term(geometry[:, span], edge_weight[...])
        picks = onehot(receivers[:, span], begin, valid[0, 0], total.shape[0])
        more(0, 8)
        hidden = []
        for part in range(parts):
            here = shift[:, part * LANES : (part + 1) * LANES]
            hidden.append(silu_half(rows[pl.ds(part, tile, stride=parts), :] + here))
            more(1 + part, 8)
        more(5, 8)
        total[...] += dot(picks, jnp.concatenate(hidden, axis=1))
        more(6, 8)
        more(7, 8)

    pipeline(receivers.shape[1] // tile, fetch, work, one, two)
    gathered = dot(total[...].astype(BF16), second[...]).astype(BF16)
    node_hidden = silu(dot(gathered, first_weight[...])).astype(BF16)
    normed = layer_norm(dot(node_hidden, node_second[...]), gain[...])
    start = (static[...].astype(F32) + normed).astype(BF16)
    mesh_start[...] = start
    put_table(wide, 0, dot(start, next_source[...]))
    next_table[...] = wide[...].astype(BF16)


def encode(index, valid, strips, own_table, receivers, geometry, edge_weight, weights, static):
    nodes, width = static.shape
    parts = width // LANES
    strip = strips[0].shape[1]
    tile = pltpu.VMEM((ENCODE_TILE * parts, LANES), F32)
    return pl.pallas_call(
        encode_kernel,
        in_specs=[SMEM] * 2 + [VMEM] * 4 + [ANY] + [VMEM] * 11,
        out_specs=[VMEM, VMEM],
        out_shape=[
            jax.ShapeDtypeStruct((nodes, width), BF16),
            jax.ShapeDtypeStruct((nodes * parts, LANES), BF16),
        ],
        scratch_shapes=[
            pltpu.VMEM((own_table.shape[0] + 8 * strip * parts, LANES), F32),
            tile,
            tile,
            pltpu.VMEM((nodes, width), F32),
            pltpu.VMEM((nodes * parts, LANES), F32),
            pltpu.SemaphoreType.DMA,
        ],
        compiler_params=params(36),
        cost_estimate=cost(2 * receivers.shape[1] * width * 2 * width, 10 * MIB),
    )(
        index, valid, *strips, own_table, receivers, geometry, edge_weight,
        weights[0], weights[1], weights[2], weights[3], weights[4], weights[5], static, weights[6],
    )


def edge_shift(receivers, geometry, edge_weight, target):
    ids = lax.broadcasted_iota(jnp.int32, (target.shape[0], receivers.shape[1]), 0)
    picks = jnp.where(ids == receivers, 1.0, 0.0).astype(BF16)
    return (dot_rows(picks, target) + geometry_term(geometry, edge_weight)).astype(BF16)


def receive_kernel(
    start, target_weight, state_weight, receivers, geometry, edge_weight, shift, state, target
):
    @pl.when(pl.program_id(0) == 0)
    def _():
        target[...] = dot(start[...], target_weight[...]).astype(BF16)
        state[...] = dot(start[...], state_weight[...])

    shift[...] = edge_shift(receivers[...], geometry[...], edge_weight[...], target[...])


def receive_rest_kernel(target, receivers, geometry, edge_weight, shift_before, shift):
    shift[...] = edge_shift(receivers[...], geometry[...], edge_weight[...], target[...])


RECEIVE_TILE = 512


def whole(i):
    return 0, 0


def receive(start, target_weight, state_weight, receivers, geometry, edge_weight, tiles):
    nodes, width = start.shape
    edges = receivers.shape[1]
    tile = RECEIVE_TILE
    square = pl.BlockSpec((width, width), whole)
    return pl.pallas_call(
        receive_kernel,
        grid=(tiles,),
        in_specs=[
            pl.BlockSpec((nodes, width), whole),
            square,
            square,
            pl.BlockSpec((1, tile), lambda i: (0, i)),
            pl.BlockSpec((geometry.shape[0], tile), lambda i: (0, i)),
            pl.BlockSpec(edge_weight.shape, whole),
        ],
        out_specs=[
            pl.BlockSpec((tile, width), lambda i: (i, 0)),
            pl.BlockSpec((nodes, width), whole),
            pl.BlockSpec((nodes, width), whole),
        ],
        out_shape=[
            jax.ShapeDtypeStruct((edges, width), BF16),
            jax.ShapeDtypeStruct((nodes, width), F32),
            jax.ShapeDtypeStruct((nodes, width), BF16),
        ],
        compiler_params=params(20),
        cost_estimate=cost(2 * tiles * tile * width * 2 * width, 8 * MIB),
    )(start, target_weight, state_weight, receivers, geometry, edge_weight)


def receive_rest(target, receivers, geometry, edge_weight, shift, tiles):
    nodes, width = target.shape
    tile = RECEIVE_TILE
    rest = receivers.shape[1] // tile - tiles
    return pl.pallas_call(
        receive_rest_kernel,
        grid=(rest,),
        in_specs=[
            pl.BlockSpec((nodes, width), whole),
            pl.BlockSpec((1, tile), lambda i: (0, i + tiles)),
            pl.BlockSpec((geometry.shape[0], tile), lambda i: (0, i + tiles)),
            pl.BlockSpec(edge_weight.shape, whole),
            ANY,
        ],
        out_specs=pl.BlockSpec((tile, width), lambda i: (i + tiles, 0)),
        out_shape=jax.ShapeDtypeStruct(shift.shape, BF16),
        input_output_aliases={4: 0},
        compiler_params=params(20),
        cost_estimate=cost(2 * rest * tile * width * 2 * width, 8 * MIB),
    )(target, receivers, geometry, edge_weight, shift)


def fill_table(blocks, table):
    size = blocks[0].shape[0]
    for slot, block in enumerate(blocks):
        table[pl.ds(slot * size, size), :] = block[...].astype(F32)


PROCESS_TILE = 512


def process_kernel(
    index, valid, b0, b1, b2, b3, b4, b5, b6, b7, b8, receivers, shift, state, start, second,
    message_weight, out_weight, gain, next_source, next_table, table, one, two, total, wide,
):
    parts = second.shape[0] // LANES
    total[...] = jnp.zeros_like(total)
    fill_table((b0, b1, b2, b3, b4, b5, b6, b7, b8), table)
    tile = PROCESS_TILE

    def fetch(i, rows, piece, pieces_):
        count = tile // pieces_
        gather(index, i * tile + piece * count, count, table, rows, piece * count, parts)

    def work(i, rows, more):
        begin = pl.multiple_of(i * tile, tile)
        span = pl.ds(begin, tile)
        picks = onehot(receivers[:, span], begin, valid[0, 0], total.shape[0])
        more(0, 8)
        hidden = []
        for part in range(parts):
            here = shift[span, part * LANES : (part + 1) * LANES].astype(F32)
            hidden.append(silu_half(rows[pl.ds(part, tile, stride=parts), :] + here))
            more(1 + part, 8)
        more(5, 8)
        total[...] += dot(picks, jnp.concatenate(hidden, axis=1))
        more(6, 8)
        more(7, 8)

    pipeline(receivers.shape[1] // tile, fetch, work, one, two)
    summed = dot(total[...].astype(BF16), second[...]).astype(BF16)
    update = silu(dot(summed, message_weight[...]) + state[...]).astype(BF16)
    normed = layer_norm(dot(update, out_weight[...]), gain[...])
    end = (start[...].astype(F32) + normed).astype(BF16)
    put_table(wide, 0, dot(end, next_source[...]))
    next_table[...] = wide[...].astype(BF16)


def process(index, valid, blocks, receivers, shift, state, start, weights):
    nodes, width = start.shape
    parts = width // LANES
    edges = receivers.shape[1]
    tile = pltpu.VMEM((PROCESS_TILE * parts, LANES), F32)
    return pl.pallas_call(
        process_kernel,
        in_specs=[SMEM] * 2 + [VMEM] * 18,
        out_specs=VMEM,
        out_shape=jax.ShapeDtypeStruct((nodes * parts, LANES), BF16),
        scratch_shapes=[
            pltpu.VMEM((9 * nodes * parts, LANES), F32),
            tile,
            tile,
            pltpu.VMEM((nodes, width), F32),
            pltpu.VMEM((nodes * parts, LANES), F32),
        ],
        compiler_params=params(36),
        cost_estimate=cost(2 * edges * width * 2 * width, 12 * MIB),
    )(index, valid, *blocks, receivers, shift, state, start, *weights)


def target_kernel(embedded, weight, target):
    target[...] = dot(embedded[...], weight[...]).astype(BF16)


def grid_target(embedded, weight):
    cells, width = embedded.shape
    tile = 512
    return pl.pallas_call(
        target_kernel,
        grid=(cells // tile,),
        in_specs=[
            pl.BlockSpec((tile, width), lambda i: (i, 0)),
            pl.BlockSpec((width, width), lambda i: (0, 0)),
        ],
        out_specs=pl.BlockSpec((tile, width), lambda i: (i, 0)),
        out_shape=jax.ShapeDtypeStruct((cells, width), BF16),
        compiler_params=params(16),
        cost_estimate=cost(2 * cells * width * width, 4 * MIB),
    )(embedded, weight)


DECODE_TILE = 512


def decode_kernel(
    index, b0, b1, b2, b3, b4, b5, b6, b7, b8, target, fields, hidden_weight, output_weight,
    prediction, table, one, two, result, sems,
):
    cells, width = target.shape
    parts = width // LANES
    fill_table((b0, b1, b2, b3, b4, b5, b6, b7, b8), table)
    tile = DECODE_TILE
    tiles = cells // tile
    halves = [
        pltpu.make_async_copy(result.at[:, :, span], prediction.at[:, :, span], sems.at[i])
        for i, span in enumerate((pl.ds(0, cells // 2), pl.ds(cells // 2, cells // 2)))
    ]

    def fetch(i, rows, piece, pieces_):
        count = tile // pieces_
        for k in range(3):
            first = k * cells + i * tile + piece * count
            gather(index, first, count, table, rows, k * tile + piece * count, parts)

    def work(i, rows, more):
        begin = pl.multiple_of(i * tile, tile)
        span = pl.ds(begin, tile)
        summed = []
        for part in range(parts):
            here = target[span, part * LANES : (part + 1) * LANES].astype(F32)
            edge = [
                silu_half(rows[pl.ds(k * tile * parts + part, tile, stride=parts), :] + here)
                for k in range(3)
            ]
            total = edge[0].astype(F32) + edge[1].astype(F32) + edge[2].astype(F32)
            summed.append(total.astype(BF16))
            more(part, 8)
        more(4, 8)
        more(5, 8)
        final = silu_half(dot(jnp.concatenate(summed, axis=1), hidden_weight[...]))
        more(6, 8)
        more(7, 8)
        change = lax.dot_general(
            output_weight[...], final, (((1,), (1,)), ((), ())), preferred_element_type=F32
        )
        result[:, 0, span] = fields[:, span].astype(F32) + change

    def at_pair(pair):
        @pl.when(pair == tiles // 4)
        def _():
            halves[0].start()

    pipeline(tiles, fetch, work, one, two, at_pair)
    halves[1].start()
    halves[0].wait()
    halves[1].wait()


def decode(index, blocks, target, fields, hidden_weight, output_weight):
    cells, width = target.shape
    channels = fields.shape[0]
    parts = width // LANES
    size = blocks[0].shape[0]
    tile = pltpu.VMEM((3 * DECODE_TILE * parts, LANES), F32)
    return pl.pallas_call(
        decode_kernel,
        in_specs=[SMEM] + [VMEM] * 13,
        out_specs=HBM,
        out_shape=jax.ShapeDtypeStruct((channels, 1, cells), F32),
        scratch_shapes=[
            pltpu.VMEM((9 * size, LANES), F32),
            tile,
            tile,
            pltpu.VMEM((channels, 1, cells), F32),
            pltpu.SemaphoreType.DMA((2,)),
        ],
        compiler_params=params(36),
        cost_estimate=cost(2 * cells * width * 3 * width, 12 * MIB),
    )(index, *blocks, target, fields, hidden_weight, output_weight)


def east(values):
    count = lax.axis_size("lon")
    return lax.ppermute(values, "lon", [(i, (i + 1) % count) for i in range(count)])


def west(values):
    count = lax.axis_size("lon")
    return lax.ppermute(values, "lon", [((i + 1) % count, i) for i in range(count)])


def near(values):
    count = lax.axis_size("lat")
    return lax.ppermute(values, "lat", [(i, i ^ 1) for i in range(count)])


def far(values):
    count = lax.axis_size("lat")
    ups = [(i, i + 1) for i in range(1, count - 1, 2)]
    return lax.ppermute(values, "lat", ups + [(b, a) for a, b in ups])


def swap_strips(strip):
    w, e = east(strip), west(strip)
    band = make_band(w, strip, e)
    return w, e, far(band), near(band)


def lon_shift(values, turn):
    bands, sectors = lax.axis_size("lat"), lax.axis_size("lon")
    pairs = []
    for i in range(bands):
        step = turn if i % 2 == 0 else -turn
        pairs += [(i * sectors + j, i * sectors + (j + step) % sectors) for j in range(sectors)]
    return lax.ppermute(values, ("lat", "lon"), pairs)


def swap_blocks(block, beside=tuple):
    fore = lon_shift(block, -1)
    away = far(block)
    close = near(block)
    again, fore, work = lax.optimization_barrier((block, fore, beside()))
    aft = lon_shift(again, 1)
    corner_fore = lon_shift(away, -1)
    corner_aft = far(fore)
    blocks = block, fore, aft, away, close, corner_fore, corner_aft, near(fore), near(aft)
    return blocks, work


def slots(block, same, away, close):
    a, b = block // 3, block % 3
    is_near = (a == 0) == (lax.axis_index("lat") % 2 == 1)

    def choose(three):
        return jnp.where(b == 0, three[0], jnp.where(b == 1, three[1], three[2]))

    return jnp.where(a == 1, choose(same), jnp.where(is_near, choose(close), choose(away)))


def grid_index(senders, cells, strip, parts):
    block, offset = senders // cells, senders % cells
    slot = slots(block, (0, 0, 1), (2, 3, 4), (5, 6, 7))
    outside = cells + slot * strip + offset % strip
    return jnp.where(block == 4, offset, outside) * parts


def mesh_index(senders, nodes, parts):
    block = senders // nodes
    odd = lax.axis_index("lat") % 2 == 1
    block = jnp.where(odd, block // 3 * 3 + 2 - block % 3, block)
    slot = slots(block, (2, 0, 1), (6, 3, 5), (7, 4, 8))
    return (slot * nodes + senders % nodes) * parts


def shards(
    grid_fields,
    mesh_static,
    encode_senders,
    encode_receivers,
    encode_geometry,
    encode_valid,
    mesh_senders,
    mesh_receivers,
    mesh_geometry,
    mesh_valid,
    decode_senders,
    embed_weight,
    encode_source,
    encode_edge,
    encode_second,
    node_first,
    node_second,
    node_gain,
    process_source,
    process_target,
    process_edge,
    process_second,
    update_message,
    update_state,
    update_out,
    process_gain,
    decode_source,
    decode_target,
    decode_hidden,
    output_weight,
):
    fields = grid_fields[0, 0].T
    static = mesh_static[0, 0]
    cells, nodes, width = fields.shape[1], static.shape[0], static.shape[1]
    parts = width // LANES
    strip = cells // 8
    fields, own_strip = take_strip(fields, strip)
    strips = swap_strips(own_strip)
    encode_index = grid_index(encode_senders[0, 0], cells, strip, parts)
    process_index = mesh_index(mesh_senders[0, 0], nodes, parts)
    decode_index = mesh_index(decode_senders[0, 0].reshape(-1), nodes, parts)
    embedded, own_table = embed_own(fields, embed_weight, encode_source)
    start, table = encode(
        encode_index,
        encode_valid,
        strips,
        own_table,
        encode_receivers[0],
        encode_geometry[0, 0],
        encode_edge,
        (
            embed_weight,
            encode_source,
            encode_second,
            node_first,
            node_second,
            node_gain[None],
            process_source,
        ),
        static,
    )
    receivers, geometry = mesh_receivers[0], mesh_geometry[0, 0]
    tiles = receivers.shape[1] // RECEIVE_TILE * 5 // 8
    blocks, (shift, state, target) = swap_blocks(
        table,
        lambda: receive(
            start, process_target, update_state, receivers, geometry, process_edge, tiles
        ),
    )
    shift = receive_rest(target, receivers, geometry, process_edge, shift, tiles)
    table = process(
        process_index,
        mesh_valid,
        blocks,
        receivers,
        shift,
        state,
        start,
        (process_second, update_message, update_out, process_gain[None], decode_source),
    )
    blocks, _ = swap_blocks(table)
    target = grid_target(embedded, decode_target)
    prediction = decode(decode_index, blocks, target, fields, decode_hidden, output_weight.T)
    return prediction.transpose(1, 2, 0)[None]


def solution(mesh):
    devices = P("lat", "lon")
    in_specs = (devices,) * 11 + (P(),) * 19
    return jax.shard_map(
        shards, mesh=mesh, in_specs=in_specs, out_specs=devices, check_vma=False
    )
```
